32 devices in a mesh: ctx: 8 (over z, x), wa: 4 (over y, core).
Axes of the slice: x: 2, y: 2, z: 4, core: 2. Of those that a mesh axis runs over, the one named last changes fastest.
Arguments:
- layer_input: float32 [4, 1024, 960], P('wa', 'ctx'), may hold values from -6 to 6
- cotangent: float32 [4, 1024, 960], P('wa', 'ctx'), may hold values from -6 to 6
- block_order: int32 [4, 16], P('wa'), may hold values from 0 to 15, each once within a row
- qkv_weight: float32 [960, 1600], P('wa'), may hold values from -0.3125 to 0.3125
- qkv_first: float32 [960, 1600], P('wa'), may hold values from -112 to 112
- qkv_second: float32 [960, 1600], P('wa'), may hold values from 24.576 to 98.304
- out_weight: float32 [960, 960], P('wa'), may hold values from -0.375 to 0.375
- out_first: float32 [960, 960], P('wa'), may hold values from -32 to 32
- out_second: float32 [960, 960], P('wa'), may hold values from 2.048 to 8.192
- gate_up_weight: float32 [960, 5120], P('wa'), may hold values from -0.1875 to 0.1875
- gate_up_first: float32 [960, 5120], P('wa'), may hold values from -6 to 6
- gate_up_second: float32 [960, 5120], P('wa'), may hold values from 0.4096 to 1.6384
- down_weight: float32 [2560, 960], P('wa'), may hold values from -0.125 to 0.125
- down_first: float32 [2560, 960], P('wa'), may hold values from -28 to 28
- down_second: float32 [2560, 960], P('wa'), may hold values from 1.6384 to 6.5536
- gains: float32 [2, 960], P(None, 'wa'), may hold values from 0.5 to 1.5
- gain_first: float32 [2, 960], P(None, 'wa'), may hold values from -142.72 to 142.72
- gain_second: float32 [2, 960], P(None, 'wa'), may hold values from 2.048 to 409.6
Outputs:
- layer_output: float32 [4, 1024, 960], P('wa', 'ctx')
- input_grad: float32 [4, 1024, 960], P('wa', 'ctx')
- qkv_new: float32 [960, 1600], P('wa', 'ctx')
- qkv_first_new: float32 [960, 1600], P('wa', 'ctx')
- qkv_second_new: float32 [960, 1600], P('wa', 'ctx')
- out_new: float32 [960, 960], P('wa', 'ctx')
- out_first_new: float32 [960, 960], P('wa', 'ctx')
- out_second_new: float32 [960, 960], P('wa', 'ctx')
- gate_up_new: float32 [960, 5120], P('wa', 'ctx')
- gate_up_first_new: float32 [960, 5120], P('wa', 'ctx')
- gate_up_second_new: float32 [960, 5120], P('wa', 'ctx')
- down_new: float32 [2560, 960], P('wa', 'ctx')
- down_first_new: float32 [2560, 960], P('wa', 'ctx')
- down_second_new: float32 [2560, 960], P('wa', 'ctx')
- gains_new: float32 [2, 960], P(None, 'wa')
- gain_first_new: float32 [2, 960], P(None, 'wa')
- gain_second_new: float32 [2, 960], P(None, 'wa')
- qkv_gradient: float32 [960, 1600], P('wa', 'ctx')
- out_gradient: float32 [960, 960], P('wa', 'ctx')
- gate_up_gradient: float32 [960, 5120], P('wa', 'ctx')
- down_gradient: float32 [2560, 960], P('wa', 'ctx')
- gain_gradient: float32 [2, 960], P(None, 'wa')
The draws below stay inside these ranges and needn't reach their ends.
Inputs may be any that keep to these rules, and one draw needn't show every extreme that they name: Each row of block_order names every one of the 16 half-blocks of its sequence exactly once.
All inputs are finite; a program needn't handle non-finite values.
Results may differ from the reference program's by a relative error of at most 0.02.
The reference program's roundings to bfloat16 on the way count: a program that leaves them out, or rounds other values in their place, can miss the bound.
Values may be sent and summed in bfloat16 or wider, within the bound.
No kernel may reach another device: no remote copies, remote signals or barrier semaphores. Data moves between devices by JAX's collectives and lax.ppermute only.
A program may use at most 192 MiB of HBM per device.

```python
import math
import jax
import jax.numpy as jnp
from jax import lax

D = 960
HEADS = 15
KV_HEADS = 5
HEAD_DIM = 64
FF = 2560
TOK_DEV = 128
STEP = 10
QKV = 1600
LEN = 1024
SEQS = 4
N_CTX = 8
N_WA = 4


def gain_scales(weight_one, weight_two):
    token_total = N_WA * TOK_DEV * N_CTX
    return jnp.array([weight_one * token_total, weight_two * token_total], dtype=jnp.float32)[:, None]


def draw_gain_first(key, part):
    key = jax.random.fold_in(key, 11)
    scales = jnp.sqrt(gain_scales(25.0, 0.5)) * 0.111
    values = jnp.clip(jax.random.normal(key, (2, D), jnp.float32), -4.0, 4.0)
    return values * scales


def draw_gain_second(key, part):
    key = jax.random.fold_in(key, 12)
    factor = jnp.exp(jax.random.uniform(key, (2, D), jnp.float32, 0.0, jnp.log(4.0)))
    return factor * gain_scales(25.0, 0.5) * 0.001


def levels(rng, extent, split, smallest, high):
    factor_of, own = 1.0, jax.random.fold_in(rng, 6)
    for axis_at, shards_of in split:
        draws = jnp.exp(jax.random.uniform(jax.random.fold_in(own, axis_at), (shards_of,), jnp.float32, smallest / len(split), high / len(split)))
        factor_of = factor_of * jnp.repeat(draws, extent[axis_at] // shards_of).reshape([-1 if axis == axis_at else 1 for axis in range(len(extent))])
    return factor_of


def noise(rng, shape, scale, bound, shards=(), kind=jnp.bfloat16):
    loudness = levels(rng, shape, shards, -0.22, 0.18) if shards else 1.0
    result = jax.random.normal(rng, shape, jnp.float32) * scale * loudness
    return jnp.minimum(jnp.maximum(result, -bound), bound).astype(kind)


def setup_inputs(seed: int = 0) -> dict:
    arg_keys = jax.random.split(jax.random.key(seed), 19)
    layer_input = noise(arg_keys[0], (SEQS, LEN, D), 1.0, 6.0, ((0, 4), (1, 8)), jnp.float32)
    cotangent = noise(arg_keys[1], (SEQS, LEN, D), 1.0, 6.0, ((0, 4), (1, 8)), jnp.float32)
    block_order = jax.vmap(lambda own: jax.random.permutation(own, 2 * N_CTX))(jax.random.split(arg_keys[2], SEQS)).reshape((SEQS, 2 * N_CTX)).astype(jnp.int32)
    qkv_weight = noise(arg_keys[3], (D, QKV), (2 * D // 5) ** -0.5, 0.3125, ((0, 4),), jnp.float32)
    qkv_first = noise(arg_keys[4], (D, QKV), (0.111 * (6.0 * N_WA * TOK_DEV * N_CTX) ** 0.5), 112.0, ((0, 4),), jnp.float32)
    qkv_second = jnp.clip(jnp.exp(math.log(98.304) - 1.3862944 * jax.random.uniform(arg_keys[5], (D, QKV), jnp.float32) ** levels(arg_keys[5], (D, QKV), ((0, 4),), -0.2, 0.2)), 24.576, 98.304)
    out_weight = noise(arg_keys[6], (D, D), (D // 4) ** -0.5, 0.375, ((0, 4),), jnp.float32)
    out_first = noise(arg_keys[7], (D, D), (0.111 * (0.5 * N_WA * TOK_DEV * N_CTX) ** 0.5), 32.0, ((0, 4),), jnp.float32)
    out_second = jnp.clip(jnp.exp(math.log(8.192) - 1.3862944 * jax.random.uniform(arg_keys[8], (D, D), jnp.float32) ** levels(arg_keys[8], (D, D), ((0, 4),), -0.2, 0.2)), 2.048, 8.192)
    gate_up_weight = noise(arg_keys[9], (D, 2 * FF), D ** -0.5, 0.1875, ((0, 4),), jnp.float32)
    gate_up_first = noise(arg_keys[10], (D, 2 * FF), (0.111 * (0.1 * N_WA * TOK_DEV * N_CTX) ** 0.5), 6.0, ((0, 4),), jnp.float32)
    gate_up_second = jnp.clip(jnp.exp(math.log(1.6384) - 1.3862944 * jax.random.uniform(arg_keys[11], (D, 2 * FF), jnp.float32) ** levels(arg_keys[11], (D, 2 * FF), ((0, 4),), -0.2, 0.2)), 0.4096, 1.6384)
    down_weight = noise(arg_keys[12], (FF, D), FF ** -0.5, 0.125, ((0, 4),), jnp.float32)
    down_first = noise(arg_keys[13], (FF, D), (0.111 * (0.4 * N_WA * TOK_DEV * N_CTX) ** 0.5), 28.0, ((0, 4),), jnp.float32)
    down_second = jnp.clip(jnp.exp(math.log(6.5536) - 1.3862944 * jax.random.uniform(arg_keys[14], (FF, D), jnp.float32) ** levels(arg_keys[14], (FF, D), ((0, 4),), -0.2, 0.2)), 1.6384, 6.5536)
    gains = jnp.clip(1.0 + 0.1 * jax.random.normal(arg_keys[15], (2, D), jnp.float32), 0.5, 1.5)
    gain_first = draw_gain_first(jax.random.fold_in(arg_keys[18], 71), 0)
    gain_second = draw_gain_second(jax.random.fold_in(arg_keys[18], 71), 0)
    return {"layer_input": layer_input, "cotangent": cotangent, "block_order": block_order, "qkv_weight": qkv_weight, "qkv_first": qkv_first, "qkv_second": qkv_second, "out_weight": out_weight, "out_first": out_first, "out_second": out_second, "gate_up_weight": gate_up_weight, "gate_up_first": gate_up_first, "gate_up_second": gate_up_second, "down_weight": down_weight, "down_first": down_first, "down_second": down_second, "gains": gains, "gain_first": gain_first, "gain_second": gain_second}


NEG_FILL = -1e+30
NORM_EPS = 1e-05
THETA = 10000.0
BETA_ONE = 0.9
BETA_TWO = 0.999
ADAM_EPS = 1e-08
RATE_MATRIX = 0.05
RATE_GAIN = 0.5
WEIGHT_DECAY = 0.1
HIGH = lax.Precision.HIGHEST

@jax.custom_vjp
def low(v):
    return lax.optimization_barrier(v.astype(jnp.bfloat16)).astype(jnp.float32)

@jax.custom_vjp
def low_back(v):
    return v

def low_keep(v):
    return (low(v), None)

def low_pass(kept, grad):
    return (grad,)

def back_keep(v):
    return (v, None)

def back_low(kept, grad):
    return (low(grad),)
low.defvjp(low_keep, low_pass)
low_back.defvjp(back_keep, back_low)

def matmul(left, right):
    return jnp.dot(left, right, precision=HIGH)

def rms_norm(values, gain_row):
    return values * lax.rsqrt(lax.optimization_barrier(jnp.mean(values * values, axis=-1, keepdims=True)) + NORM_EPS) * gain_row

def rotate(values, positions):
    half_len = HEAD_DIM // 2
    freq_table = THETA ** (-jnp.arange(half_len, dtype=jnp.float32) / half_len)
    angle_table = positions.astype(jnp.float32)[:, None] * freq_table[None, :]
    cos_table = jnp.cos(angle_table)[:, None, :]
    sin_table = jnp.sin(angle_table)[:, None, :]
    leading = values[..., :half_len]
    trailing = values[..., half_len:]
    return jnp.concatenate([leading * cos_table - trailing * sin_table, trailing * cos_table + leading * sin_table], axis=-1)

def attention(query, keys, values, positions):
    group = HEADS // KV_HEADS
    blocks = LEN // TOK_DEV
    query = query.reshape(blocks, TOK_DEV, KV_HEADS, group, HEAD_DIM)
    query_pos = positions.reshape(blocks, TOK_DEV)

    def one_block(pair):
        query_block, pos_block = pair
        scores = jnp.einsum('qkgd,tkd->kgqt', query_block, keys, precision=HIGH) * HEAD_DIM ** (-0.5)
        scores = low_back(scores)
        visible = positions[None, :] <= pos_block[:, None]
        scores = jnp.where(visible, scores, NEG_FILL)
        probs = low(jax.nn.softmax(scores, axis=-1))
        return jnp.einsum('kgqt,tkd->qkgd', probs, values, precision=HIGH)
    outputs = lax.map(jax.checkpoint(one_block), (query, query_pos))
    return outputs.reshape(LEN, HEADS * HEAD_DIM)

def forward_layer(tokens, qkv_weight, out_weight, gate_up_weight, down_weight, gains, positions):
    gains_low = low(gains)
    qkv_low = low(qkv_weight)
    out_low = low(out_weight)
    gate_up_low = low(gate_up_weight)
    down_low = low(down_weight)
    query_width = HEADS * HEAD_DIM
    pair_width = KV_HEADS * HEAD_DIM
    norm_one = rms_norm(tokens, gains_low[0])
    projected = low_back(matmul(low(norm_one), qkv_low))
    query = rotate(projected[:, :query_width].reshape(LEN, HEADS, HEAD_DIM), positions)
    keys = rotate(projected[:, query_width:query_width + pair_width].reshape(LEN, KV_HEADS, HEAD_DIM), positions)
    values = projected[:, query_width + pair_width:].reshape(LEN, KV_HEADS, HEAD_DIM)
    attn = attention(low(query), low(keys), low(values), positions)
    attn = low_back(low(attn))
    residual = tokens + low_back(matmul(attn, out_low))
    norm_two = rms_norm(residual, gains_low[1])
    gate_up = low_back(matmul(low(norm_two), gate_up_low))
    gate = gate_up[:, :FF]
    up_part = gate_up[:, FF:]
    inner = low(jax.nn.silu(gate) * up_part)
    return residual + low_back(matmul(inner, down_low))

def adamw(weight, moment_one, moment_two, gradient, step_rate, decay_rate):
    first_new = BETA_ONE * moment_one + (1.0 - BETA_ONE) * gradient
    second_new = BETA_TWO * moment_two + (1.0 - BETA_TWO) * gradient * gradient
    first_hat = first_new / (1.0 - BETA_ONE ** STEP)
    second_hat = second_new / (1.0 - BETA_TWO ** STEP)
    weight_new = weight - step_rate * (first_hat / (jnp.sqrt(second_hat) + ADAM_EPS) + decay_rate * weight)
    return (weight_new, first_new, second_new)

def reference(layer_input, cotangent, block_order, qkv_weight, qkv_first, qkv_second, out_weight, out_first, out_second, gate_up_weight, gate_up_first, gate_up_second, down_weight, down_first, down_second, gains, gain_first, gain_second):
    half_len = TOK_DEV // 2
    weights = (qkv_weight, out_weight, gate_up_weight, down_weight, gains)

    def one_sequence(sums, item):
        tokens, upstream, order_row = item
        offsets = jnp.arange(half_len, dtype=jnp.int32)
        positions = (order_row[:, None] * half_len + offsets[None, :]).reshape(-1).astype(jnp.int32)

        def layer(tok_rows, qkv_mat, out_mat, gate_up_mat, down_mat, gain_rows):
            return forward_layer(tok_rows, qkv_mat, out_mat, gate_up_mat, down_mat, gain_rows, positions)
        output, pullback = jax.vjp(layer, tokens, *weights)
        grads = pullback(upstream)
        sums = tuple((running + piece_grad for running, piece_grad in zip(sums, grads[1:])))
        return (sums, (output, grads[0]))
    zeros = tuple((jnp.zeros_like(weight) for weight in weights))
    sums, outputs = lax.scan(one_sequence, zeros, (layer_input, cotangent, block_order))
    layer_output, input_grad = outputs
    qkv_new, qkv_first_new, qkv_second_new = adamw(qkv_weight, qkv_first, qkv_second, sums[0], RATE_MATRIX, WEIGHT_DECAY)
    out_new, out_first_new, out_second_new = adamw(out_weight, out_first, out_second, sums[1], RATE_MATRIX, WEIGHT_DECAY)
    gate_up_new, gate_up_first_new, gate_up_second_new = adamw(gate_up_weight, gate_up_first, gate_up_second, sums[2], RATE_MATRIX, WEIGHT_DECAY)
    down_new, down_first_new, down_second_new = adamw(down_weight, down_first, down_second, sums[3], RATE_MATRIX, WEIGHT_DECAY)
    gains_new, gain_first_new, gain_second_new = adamw(gains, gain_first, gain_second, sums[4], RATE_GAIN, 0.0)
    return (layer_output, input_grad, qkv_new, qkv_first_new, qkv_second_new, out_new, out_first_new, out_second_new, gate_up_new, gate_up_first_new, gate_up_second_new, down_new, down_first_new, down_second_new, gains_new, gain_first_new, gain_second_new, sums[0], sums[1], sums[2], sums[3], sums[4])
```

```python
import functools

import jax
import jax.numpy as jnp
from jax import lax
from jax.experimental import pallas as pl
from jax.experimental.pallas import tpu as pltpu
from jax.sharding import PartitionSpec as P

HEADS = 15
KV_HEADS = 5
GROUP = HEADS // KV_HEADS
HEAD_DIM = 64
PAIR = 2 * HEAD_DIM
FF = 2560
STEP = 10
SHARE = 4

NEG_FILL = -1e30
NORM_EPS = 1e-05
THETA = 10000.0
BETA_ONE = 0.9
BETA_TWO = 0.999
ADAM_EPS = 1e-08
RATE_MATRIX = 0.05
RATE_GAIN = 0.5
WEIGHT_DECAY = 0.1
BF16 = jnp.bfloat16
F32 = jnp.float32


def matmul(left, right):
    return jnp.dot(left, right, preferred_element_type=F32)


def flip(value, axis, bit):
    count = lax.axis_size(axis)
    return lax.ppermute(value, axis, [(i, i ^ bit) for i in range(count)])


def bits_of(count, first=1):
    bits = []
    while first < count:
        bits.append(first)
        first *= 2
    return bits


def gather_ordered(value, axis):
    rank = lax.axis_index(axis)
    blocks = {0: value}
    for bit in reversed(bits_of(lax.axis_size(axis))):
        upper = (rank & bit) != 0
        merged = {}
        for key, block in blocks.items():
            other = flip(block, axis, bit)
            merged[key] = jnp.where(upper, other, block)
            merged[key | bit] = jnp.where(upper, block, other)
        blocks = merged
    return [blocks[key] for key in sorted(blocks)]


def gather_relative(value, axis):
    blocks = {0: value}
    for bit in reversed(bits_of(lax.axis_size(axis))):
        blocks.update({key | bit: flip(block, axis, bit) for key, block in blocks.items()})
    return [blocks[key] for key in sorted(blocks)]


def halve(pieces, dim, axis, bits, place):
    rank = lax.axis_index(axis)
    for bit, part_bit in zip(bits, place):
        shape = pieces.shape
        low = part_bit
        high = shape[dim] // (2 * low)
        split = pieces.reshape(shape[:dim] + (high, 2, low) + shape[dim + 1 :])
        side = ((rank & bit) != 0).astype(jnp.int32)
        mine = lax.dynamic_index_in_dim(split, side, dim + 1, keepdims=False)
        other = lax.dynamic_index_in_dim(split, 1 - side, dim + 1, keepdims=False)
        got = flip(other, axis, bit)
        pieces = (mine.astype(F32) + got.astype(F32)).astype(BF16)
        pieces = pieces.reshape(shape[:dim] + (high * low,) + shape[dim + 1 :])
    return pieces


def scatter_sum(pieces, dim, axis, bits=None):
    count = lax.axis_size(axis)
    bits = bits_of(count) if bits is None else bits
    return halve(pieces, dim, axis, bits, [1] * len(bits)).squeeze(dim)


def ring_order(count):
    return list(range(0, count, 2)) + list(range(count - 1, 0, -2))


def ring_send(value, steps):
    ring = ring_order(lax.axis_size("ctx"))
    count = len(ring)
    return lax.ppermute(
        value, "ctx", [(ring[i], ring[(i + steps) % count]) for i in range(count)]
    )


def ring_gather(block):
    count = lax.axis_size("ctx")
    blocks = {0: block}
    ahead = behind = block
    half = block.shape[0] // 2
    for step in range(1, count // 2):
        ahead, behind = ring_send(ahead, -1), ring_send(behind, 1)
        blocks[step], blocks[count - step] = ahead, behind
    blocks[count // 2] = jnp.concatenate([ring_send(ahead[:half], -1), ring_send(behind[half:], 1)])
    return [blocks[k] for k in range(count)]


def ring_reduce(parts):
    count = lax.axis_size("ctx")
    middle = parts(count // 2)
    half = middle.shape[0] // 2
    ahead = ring_send(middle[:half], 1)
    behind = ring_send(middle[half:], -1)
    for k in range(count // 2 - 1, 0, -1):
        one, two = parts(k), parts(count - k)
        if k == count // 2 - 1:
            one = jnp.concatenate([(one[:half].astype(F32) + ahead).astype(BF16), one[half:]])
            two = jnp.concatenate([two[:half], (two[half:].astype(F32) + behind).astype(BF16)])
        else:
            one = (one.astype(F32) + ahead).astype(BF16)
            two = (two.astype(F32) + behind).astype(BF16)
        ahead, behind = ring_send(one, 1), ring_send(two, -1)
    return parts(0).astype(F32) + ahead.astype(F32) + behind.astype(F32)


def share_gather(block):
    half = block.shape[0] // 2
    rows = []
    for part, (first, second) in ((block[:half], (1, 2)), (block[half:], (2, 1))):
        pair = jnp.stack([part, flip(part, "ctx", first)])
        rows.append(jnp.concatenate([pair, flip(pair, "ctx", second)]))
    stacked = jnp.concatenate(rows)
    return stacked.reshape((2 * SHARE * half,) + block.shape[1:])


def share_reduce(rows):
    half = rows.shape[0] // (2 * SHARE)
    stacked = rows.reshape((2, 2, 2, half) + rows.shape[1:])
    sums = []
    for part, (first, second) in ((stacked[0], (2, 1)), (stacked[1], (1, 2))):
        got = flip(part[1].astype(BF16), "ctx", first)
        pair = part[0] + got.astype(F32)
        got = flip(pair[1].astype(BF16), "ctx", second)
        sums.append(pair[0] + got.astype(F32))
    return jnp.concatenate(sums)


def swap_places(value):
    count, shards = lax.axis_size("ctx"), lax.axis_size("wa")
    pairs = []
    for ctx in range(count):
        for own in range(shards):
            high, low = ctx // SHARE, ctx % SHARE
            pairs.append((ctx * shards + own, (high * SHARE + own) * shards + low))
    return lax.ppermute(value, ("ctx", "wa"), pairs)


def dot_t(left, right):
    return lax.dot_general(left, right, (((1,), (1,)), ((), ())), preferred_element_type=F32)


def t_dot(left, right):
    return lax.dot_general(left, right, (((0,), (0,)), ((), ())), preferred_element_type=F32)


def attend_kernel(q_ref, kv_ref, qpos_ref, kpos_ref, out_ref, lse_ref, max_ref, sum_ref, acc_ref):
    chunk = pl.program_id(1)

    @pl.when(chunk == 0)
    def _():
        max_ref[...] = jnp.full_like(max_ref, NEG_FILL)
        sum_ref[...] = jnp.zeros_like(sum_ref)
        acc_ref[...] = jnp.zeros_like(acc_ref)

    kv = kv_ref[...]
    scores = dot_t(q_ref[0], kv)
    visible = kpos_ref[0] <= qpos_ref[...]
    scores = jnp.where(visible, scores, NEG_FILL)
    top = jnp.maximum(max_ref[...], jnp.max(scores, axis=1, keepdims=True))
    probs = jnp.where(visible, jnp.exp(scores - top), 0.0)
    factor = jnp.exp(max_ref[...] - top)
    max_ref[...] = top
    sum_ref[...] = factor * sum_ref[...] + jnp.sum(probs, axis=1, keepdims=True)
    acc_ref[...] = factor * acc_ref[...] + matmul(probs.astype(BF16), kv)

    @pl.when(chunk == pl.num_programs(1) - 1)
    def _():
        out_ref[0] = acc_ref[...] / sum_ref[...]
        lse_ref[0] = max_ref[...] + jnp.log(sum_ref[...])


def attend_back_kernel(
    q_ref, do_ref, kv_ref, out_ref, lse_ref, qpos_ref, kpos_ref, dq_ref, dkv_ref, acc_ref
):
    chunk = pl.program_id(1)

    @pl.when(chunk == 0)
    def _():
        acc_ref[...] = jnp.zeros_like(acc_ref)

    kv, query, out_grad = kv_ref[...], q_ref[0], do_ref[0]
    delta = jnp.sum(out_grad.astype(F32) * out_ref[0], axis=1, keepdims=True)
    visible = kpos_ref[0] <= qpos_ref[...]
    probs = jnp.where(visible, jnp.exp(dot_t(query, kv) - lse_ref[0]), 0.0)
    score_grad = (probs * (dot_t(out_grad, kv) - delta)).astype(BF16)
    acc_ref[...] += matmul(score_grad, kv)
    dkv = t_dot(score_grad, query) + t_dot(probs.astype(BF16), out_grad)
    dkv_ref[...] = dkv.astype(BF16)

    @pl.when(chunk == pl.num_programs(1) - 1)
    def _():
        dq_ref[0] = acc_ref[...]


def attention_specs(rows, keys):
    width = min(keys, 1024)
    by_head = pl.BlockSpec((1, rows, PAIR), lambda g, c: (g, 0, 0))
    by_keys = pl.BlockSpec((width, PAIR), lambda g, c: (c, g))
    column = pl.BlockSpec((1, rows, 1), lambda g, c: (g, 0, 0))
    qpos = pl.BlockSpec((rows, 1), lambda g, c: (0, 0))
    kpos = pl.BlockSpec((1, 1, width), lambda g, c: (c, 0, 0))
    return width, by_head, by_keys, column, qpos, kpos


def attend(query, pairs, query_pos, key_pos):
    rows, keys = query.shape[1], pairs.shape[0]
    width, by_head, by_keys, column, qpos, kpos = attention_specs(rows, keys)
    return pl.pallas_call(
        attend_kernel,
        grid=(KV_HEADS, keys // width),
        in_specs=[by_head, by_keys, qpos, kpos],
        out_specs=[by_head, column],
        out_shape=[
            jax.ShapeDtypeStruct((KV_HEADS, rows, PAIR), F32),
            jax.ShapeDtypeStruct((KV_HEADS, rows, 1), F32),
        ],
        scratch_shapes=[
            pltpu.VMEM((rows, 1), F32),
            pltpu.VMEM((rows, 1), F32),
            pltpu.VMEM((rows, PAIR), F32),
        ],
        compiler_params=pltpu.CompilerParams(vmem_limit_bytes=40 * 2**20),
        name="attend",
    )(query, pairs, query_pos, key_pos.reshape(keys // width, 1, width))


def attend_back(query, out_grad, pairs, out, lse, query_pos, key_pos):
    rows, keys = query.shape[1], pairs.shape[0]
    width, by_head, by_keys, column, qpos, kpos = attention_specs(rows, keys)
    return pl.pallas_call(
        attend_back_kernel,
        grid=(KV_HEADS, keys // width),
        in_specs=[by_head, by_head, by_keys, by_head, column, qpos, kpos],
        out_specs=[by_head, by_keys],
        out_shape=[
            jax.ShapeDtypeStruct((KV_HEADS, rows, PAIR), F32),
            jax.ShapeDtypeStruct(pairs.shape, BF16),
        ],
        scratch_shapes=[pltpu.VMEM((rows, PAIR), F32)],
        compiler_params=pltpu.CompilerParams(vmem_limit_bytes=40 * 2**20),
        name="attend_back",
    )(query, out_grad, pairs, out, lse, query_pos, key_pos.reshape(keys // width, 1, width))


def rotation(positions):
    half_len = HEAD_DIM // 2
    freq_table = THETA ** (-jnp.arange(half_len, dtype=F32) / half_len)
    angle_table = positions.astype(F32)[:, None] * freq_table[None, :]
    return (jnp.cos(angle_table)[:, None, :], jnp.sin(angle_table)[:, None, :])


def rotate(values, cos_table, sin_table):
    half_len = values.shape[-1] // 2
    leading = values[..., :half_len]
    trailing = values[..., half_len:]
    return jnp.concatenate(
        [leading * cos_table - trailing * sin_table, trailing * cos_table + leading * sin_table],
        axis=-1,
    )


def rotate_back(values, cos_table, sin_table):
    return rotate(values, cos_table, -sin_table)


def rms_forward(values, gain_row):
    inv_root = lax.rsqrt(jnp.mean(values * values, axis=-1, keepdims=True) + NORM_EPS)
    return (values * inv_root * gain_row, inv_root)


def rms_backward(values, inv_root, gain_row, grad_out):
    scaled = gain_row * grad_out
    return inv_root * scaled - values * inv_root**3 * jnp.mean(
        scaled * values, axis=-1, keepdims=True
    )


def adamw(weight, moment_one, moment_two, gradient, step_rate, decay_rate):
    first_new = BETA_ONE * moment_one + (1.0 - BETA_ONE) * gradient
    second_new = BETA_TWO * moment_two + (1.0 - BETA_TWO) * gradient * gradient
    first_hat = first_new / (1.0 - BETA_ONE**STEP)
    second_hat = second_new / (1.0 - BETA_TWO**STEP)
    weight_new = weight - step_rate * (
        first_hat / (jnp.sqrt(second_hat) + ADAM_EPS) + decay_rate * weight
    )
    return (weight_new, first_new, second_new)


def own_columns(array, ctx_rank, ctx_count):
    col_width = array.shape[1] // ctx_count
    return lax.dynamic_slice_in_dim(array, ctx_rank * col_width, col_width, 1)


def local(
    layer_input,
    cotangent,
    block_order,
    qkv_weight,
    qkv_first,
    qkv_second,
    out_weight,
    out_first,
    out_second,
    gate_up_weight,
    gate_up_first,
    gate_up_second,
    down_weight,
    down_first,
    down_second,
    gains,
    gain_first,
    gain_second,
):
    ctx_rank = lax.axis_index("ctx")
    ctx_count = lax.axis_size("ctx")
    wa_rank = lax.axis_index("wa")
    wa_count = lax.axis_size("wa")
    place = ctx_rank % SHARE
    tokens = layer_input[0]
    upstream = cotangent[0]
    tok_rows, width = tokens.shape
    shard = width // wa_count
    hidden = FF // SHARE
    query_width = HEADS * HEAD_DIM
    pair_width = KV_HEADS * HEAD_DIM
    half_len = tok_rows // 2

    qkv_low = qkv_weight.astype(BF16)
    gain_norm = lax.all_gather(gains.astype(BF16), "wa", axis=1, tiled=True).astype(F32)
    qkv_full = jnp.concatenate(gather_ordered(qkv_low, "wa"))
    out_full = lax.all_gather(out_weight.astype(BF16), "wa", axis=0, tiled=True)
    gate_up_part = lax.dynamic_index_in_dim(
        gate_up_weight.reshape(shard, 2, SHARE, hidden), place, 2, keepdims=False
    )
    gate_up_own = lax.all_gather(
        gate_up_part.reshape(shard, 2 * hidden).astype(BF16), "wa", axis=0, tiled=True
    )
    down_piece = lax.dynamic_index_in_dim(
        down_weight.reshape(SHARE, FF // wa_count // SHARE, width), place, 0, keepdims=False
    )
    down_own = lax.all_gather(swap_places(down_piece.astype(BF16)), "wa", axis=0, tiled=True)
    cot_low = upstream.astype(BF16)
    cot_all = share_gather(cot_low)

    ring = jnp.array(ring_order(ctx_count), jnp.int32)
    ring_place = jnp.argsort(ring).astype(jnp.int32)[ctx_rank]
    order = block_order[0].reshape(ctx_count, 2)
    offsets = jnp.arange(half_len, dtype=jnp.int32)
    key_starts = order[ring[(ring_place + jnp.arange(ctx_count)) % ctx_count]]
    key_pos = (key_starts[:, :, None] * half_len + offsets).reshape(-1)
    own_pos = key_pos[:tok_rows]
    query_pos = jnp.tile(own_pos, GROUP)[:, None]
    cos_table, sin_table = rotation(own_pos)

    norm_one, root_one = rms_forward(tokens, gain_norm[0])
    norm_one_low = norm_one.astype(BF16)
    projected = matmul(norm_one_low, qkv_full)
    query = rotate(
        projected[:, :query_width].reshape(tok_rows, HEADS, HEAD_DIM), cos_table, sin_table
    )
    keys = rotate(
        projected[:, query_width : query_width + pair_width].reshape(tok_rows, KV_HEADS, HEAD_DIM),
        cos_table,
        sin_table,
    )
    values = projected[:, query_width + pair_width :].reshape(tok_rows, KV_HEADS, HEAD_DIM)
    pair_low = jnp.concatenate([keys, values], axis=-1).astype(BF16)
    pairs = jnp.concatenate(ring_gather(pair_low.reshape(tok_rows, KV_HEADS * PAIR)))

    def by_head(rows, before, after):
        rows = rows.reshape(tok_rows, KV_HEADS, GROUP, HEAD_DIM).transpose(1, 2, 0, 3)
        rows = rows.reshape(KV_HEADS, GROUP * tok_rows, HEAD_DIM)
        return jnp.pad(rows, ((0, 0), (0, 0), (before, after)))

    def by_token(heads):
        heads = heads.reshape(KV_HEADS, GROUP, tok_rows, HEAD_DIM).transpose(2, 0, 1, 3)
        return heads.reshape(tok_rows, query_width)

    query_low = by_head(query.astype(BF16) * BF16(HEAD_DIM**-0.5), 0, HEAD_DIM)
    attn, log_total = attend(query_low, pairs, query_pos, key_pos)
    attn_low = by_token(attn[:, :, HEAD_DIM:]).astype(BF16)
    residual = tokens + matmul(attn_low, out_full)
    norm_two, root_two = rms_forward(residual, gain_norm[1])

    norm_two_all = share_gather(norm_two.astype(BF16))
    gate_up = matmul(norm_two_all, gate_up_own)
    gate = gate_up[:, :hidden]
    up_part = gate_up[:, hidden:]
    sigma = jax.nn.sigmoid(gate)
    activated = gate * sigma
    inner_low = (activated * up_part).astype(BF16)
    inner_grad = dot_t(cot_all, down_own)
    gate_grad = inner_grad * up_part * sigma * (1.0 + gate * (1.0 - sigma))
    up_grad = inner_grad * activated
    gate_up_grad_low = jnp.concatenate([gate_grad, up_grad], axis=1).astype(BF16)
    norm_two_grad = share_reduce(dot_t(gate_up_grad_low, gate_up_own))
    layer_output = residual + share_reduce(matmul(inner_low, down_own))

    gate_up_sum = t_dot(norm_two_all, gate_up_grad_low).astype(BF16)
    gate_up_sum = gate_up_sum.reshape(wa_count, shard, 2 * hidden)
    gate_up_sum = scatter_sum(gate_up_sum, 0, "wa")
    high_bits = bits_of(ctx_count, SHARE)
    groups = ctx_count // SHARE
    part_cols = 2 * FF // ctx_count
    gate_up_sum = gate_up_sum.reshape(shard, groups, part_cols).transpose(1, 0, 2)
    gate_up_sum = scatter_sum(gate_up_sum, 0, "ctx", high_bits)
    moves = []
    for ctx in range(ctx_count):
        high, low = ctx // SHARE, ctx % SHARE
        per_half = groups // 2
        moves.append((ctx, ((high // per_half) * SHARE + low) * per_half + high % per_half))
    if any(source != target for source, target in moves):
        gate_up_sum = lax.ppermute(gate_up_sum, "ctx", moves)
    gate_up_sum = gate_up_sum.astype(F32)
    down_sum = t_dot(cot_all, inner_low).astype(BF16)
    down_sum = down_sum.reshape(groups, wa_count, width // ctx_count, hidden)
    down_sum = scatter_sum(down_sum, 1, "wa")
    down_sum = scatter_sum(down_sum, 0, "ctx", high_bits)
    down_sum = swap_places(down_sum).astype(F32).T

    res_part = rms_backward(residual, root_two, gain_norm[1], norm_two_grad)
    gain_two_grad = jnp.sum(norm_two_grad * residual * root_two, axis=0)
    residual_grad = upstream + res_part
    res_low = residual_grad.astype(BF16)
    attn_grad_low = by_head(dot_t(res_low, out_full).astype(BF16), HEAD_DIM, 0)
    query_grad, pair_grad = attend_back(
        query_low, attn_grad_low, pairs, attn, log_total, query_pos, key_pos
    )
    pair_sum = ring_reduce(lambda k: pair_grad[k * tok_rows : (k + 1) * tok_rows])
    pair_sum = pair_sum.reshape(tok_rows, KV_HEADS, PAIR)
    query_grad = by_token(query_grad[:, :, :HEAD_DIM]).reshape(tok_rows, HEADS, HEAD_DIM)
    query_pre = rotate_back(query_grad * HEAD_DIM**-0.5, cos_table, sin_table)
    key_pre = rotate_back(pair_sum[:, :, :HEAD_DIM], cos_table, sin_table)
    projected_grad_low = jnp.concatenate(
        [
            query_pre.reshape(tok_rows, query_width),
            key_pre.reshape(tok_rows, pair_width),
            pair_sum[:, :, HEAD_DIM:].reshape(tok_rows, pair_width),
        ],
        axis=1,
    ).astype(BF16)
    norm_one_grad = dot_t(projected_grad_low, qkv_full)
    input_grad = residual_grad + rms_backward(tokens, root_one, gain_norm[0], norm_one_grad)

    out_cols = width // ctx_count
    out_parts = jnp.einsum(
        "td,tnc->ndc",
        attn_low,
        res_low.reshape(tok_rows, ctx_count, out_cols),
        preferred_element_type=F32,
    )
    gain_column = jnp.broadcast_to(gain_two_grad[None, :, None], (ctx_count, width, 1))
    out_parts = jnp.concatenate([out_parts, gain_column], axis=2).astype(BF16)
    out_parts = out_parts.reshape(ctx_count, wa_count, shard, out_cols + 1)
    out_parts = scatter_sum(scatter_sum(out_parts, 1, "wa"), 0, "ctx").astype(F32)
    out_sum, gain_two_sum = out_parts[:, :out_cols], out_parts[:, out_cols]

    qkv_cols = qkv_weight.shape[1] // ctx_count
    norm_shards = norm_one_low.reshape(tok_rows, wa_count, shard)
    norm_rows = jnp.concatenate(
        [
            flip(lax.dynamic_index_in_dim(norm_shards, wa_rank ^ k, 1, keepdims=False), "wa", k)
            if k
            else lax.dynamic_index_in_dim(norm_shards, wa_rank, 1, keepdims=False)
            for k in range(wa_count)
        ]
    )
    grad_rows = jnp.concatenate(gather_relative(projected_grad_low, "wa"))
    qkv_parts = jnp.einsum(
        "td,tnc->ndc",
        norm_rows,
        grad_rows.reshape(wa_count * tok_rows, ctx_count, qkv_cols),
        preferred_element_type=F32,
    )
    weight_parts = qkv_low.reshape(shard, ctx_count, qkv_cols).transpose(1, 0, 2).astype(F32)
    gain_one_rows = jnp.sum(qkv_parts * weight_parts, axis=(0, 2))
    own_gain = gains[0].astype(BF16).astype(F32)
    gain_column = jnp.broadcast_to((gain_one_rows / own_gain)[None, :, None], (ctx_count, shard, 1))
    qkv_parts = jnp.concatenate([qkv_parts, gain_column], axis=2).astype(BF16)
    qkv_parts = scatter_sum(qkv_parts, 0, "ctx").astype(F32)
    qkv_sum, gain_one_sum = qkv_parts[:, :qkv_cols], qkv_parts[:, qkv_cols]
    gain_sum = jnp.stack([gain_one_sum, gain_two_sum])

    updates = []
    for weight, first, second, gradient in (
        (qkv_weight, qkv_first, qkv_second, qkv_sum),
        (out_weight, out_first, out_second, out_sum),
        (gate_up_weight, gate_up_first, gate_up_second, gate_up_sum),
        (down_weight, down_first, down_second, down_sum),
    ):
        slices = [own_columns(array, ctx_rank, ctx_count) for array in (weight, first, second)]
        updates += adamw(*slices, gradient, RATE_MATRIX, WEIGHT_DECAY)
    updates += adamw(gains, gain_first, gain_second, gain_sum, RATE_GAIN, 0.0)
    return (
        layer_output[None],
        input_grad[None],
        *updates,
        qkv_sum,
        out_sum,
        gate_up_sum,
        down_sum,
        gain_sum,
    )


def solution(mesh):
    rows = P("wa", None)
    tokens = P("wa", "ctx", None)
    piece = P("wa", "ctx")
    gain = P(None, "wa")
    return jax.shard_map(
        local,
        mesh=mesh,
        in_specs=(tokens, tokens) + (rows,) * 13 + (gain,) * 3,
        out_specs=(tokens, tokens) + (piece,) * 12 + (gain,) * 3 + (piece,) * 4 + (gain,),
        check_vma=False,
    )
```

```python
import functools

import jax
import jax.numpy as jnp
from jax import lax
from jax.experimental import pallas as pl
from jax.experimental.pallas import tpu as pltpu
from jax.sharding import PartitionSpec as P

HEADS = 15
KV_HEADS = 5
GROUP = HEADS // KV_HEADS
HEAD_DIM = 64
PAIR = 2 * HEAD_DIM
FF = 2560
STEP = 10
SHARE = 4

NEG_FILL = -1e30
NORM_EPS = 1e-05
THETA = 10000.0
BETA_ONE = 0.9
BETA_TWO = 0.999
ADAM_EPS = 1e-08
RATE_MATRIX = 0.05
RATE_GAIN = 0.5
WEIGHT_DECAY = 0.1
BF16 = jnp.bfloat16
F32 = jnp.float32


def matmul(left, right):
    return jnp.dot(left, right, preferred_element_type=F32)


def flip(value, axis, bit):
    count = lax.axis_size(axis)
    return lax.ppermute(value, axis, [(i, i ^ bit) for i in range(count)])


def bits_of(count, first=1):
    bits = []
    while first < count:
        bits.append(first)
        first *= 2
    return bits


def gather_relative(value, axis):
    blocks = {0: value}
    for bit in reversed(bits_of(lax.axis_size(axis))):
        blocks.update({key | bit: flip(block, axis, bit) for key, block in blocks.items()})
    return [blocks[key] for key in sorted(blocks)]


def in_order(blocks, axis):
    rank = lax.axis_index(axis)
    rows = blocks[0].shape[0]
    whole = jnp.zeros((len(blocks) * rows,) + blocks[0].shape[1:], blocks[0].dtype)
    for key, block in enumerate(blocks):
        whole = lax.dynamic_update_slice_in_dim(whole, block, (rank ^ key) * rows, 0)
    return whole


def halve(pieces, dim, axis, bits, place):
    rank = lax.axis_index(axis)
    for bit, part_bit in zip(bits, place):
        shape = pieces.shape
        low = part_bit
        high = shape[dim] // (2 * low)
        split = pieces.reshape(shape[:dim] + (high, 2, low) + shape[dim + 1 :])
        side = ((rank & bit) != 0).astype(jnp.int32)
        mine = lax.dynamic_index_in_dim(split, side, dim + 1, keepdims=False)
        other = lax.dynamic_index_in_dim(split, 1 - side, dim + 1, keepdims=False)
        got = flip(other, axis, bit)
        pieces = (mine.astype(F32) + got.astype(F32)).astype(BF16)
        pieces = pieces.reshape(shape[:dim] + (high * low,) + shape[dim + 1 :])
    return pieces


def scatter_sum(pieces, dim, axis, bits=None):
    count = lax.axis_size(axis)
    bits = bits_of(count) if bits is None else bits
    return halve(pieces, dim, axis, bits, [1] * len(bits)).squeeze(dim)


def ring_order(count):
    return list(range(0, count, 2)) + list(range(count - 1, 0, -2))


def ring_send(value, steps):
    ring = ring_order(lax.axis_size("ctx"))
    count = len(ring)
    return lax.ppermute(
        value, "ctx", [(ring[i], ring[(i + steps) % count]) for i in range(count)]
    )


def ring_gather(block):
    count = lax.axis_size("ctx")
    blocks = {0: block}
    ahead = behind = block
    half = block.shape[0] // 2
    for step in range(1, count // 2):
        ahead, behind = ring_send(ahead, -1), ring_send(behind, 1)
        blocks[step], blocks[count - step] = ahead, behind
    blocks[count // 2] = jnp.concatenate([ring_send(ahead[:half], -1), ring_send(behind[half:], 1)])
    return [blocks[k] for k in range(count)]


def ring_reduce(parts):
    count = lax.axis_size("ctx")
    middle = parts(count // 2)
    half = middle.shape[0] // 2
    ahead = ring_send(middle[:half], 1)
    behind = ring_send(middle[half:], -1)
    for k in range(count // 2 - 1, 0, -1):
        one, two = parts(k), parts(count - k)
        if k == count // 2 - 1:
            one = jnp.concatenate([(one[:half].astype(F32) + ahead).astype(BF16), one[half:]])
            two = jnp.concatenate([two[:half], (two[half:].astype(F32) + behind).astype(BF16)])
        else:
            one = (one.astype(F32) + ahead).astype(BF16)
            two = (two.astype(F32) + behind).astype(BF16)
        ahead, behind = ring_send(one, 1), ring_send(two, -1)
    return parts(0).astype(F32) + ahead.astype(F32) + behind.astype(F32)


def share_gather(block):
    return [block] + [flip(block, "ctx", k) for k in range(1, SHARE)]


def share_send(parts):
    return [flip(part, "ctx", k + 1) for k, part in enumerate(parts)]


def swap_places(value):
    count, shards = lax.axis_size("ctx"), lax.axis_size("wa")
    pairs = []
    for ctx in range(count):
        for own in range(shards):
            high, low = ctx // SHARE, ctx % SHARE
            pairs.append((ctx * shards + own, (high * SHARE + own) * shards + low))
    return lax.ppermute(value, ("ctx", "wa"), pairs)


def dot_t(left, right):
    return lax.dot_general(left, right, (((1,), (1,)), ((), ())), preferred_element_type=F32)


def t_dot(left, right):
    return lax.dot_general(left, right, (((0,), (0,)), ((), ())), preferred_element_type=F32)


def lanes(rows):
    return lax.broadcasted_iota(jnp.int32, (rows, PAIR), 1)


def place_head(tile, odd, upper):
    if odd != upper:
        tile = pltpu.roll(tile, HEAD_DIM, 1)
    half = lanes(tile.shape[0]) >= HEAD_DIM
    return jnp.where(half if upper else jnp.logical_not(half), tile, 0.0)


def turn(tile, cos, sin):
    half = HEAD_DIM // 2
    leading = (lanes(tile.shape[0]) % HEAD_DIM) < half
    partner = jnp.where(leading, pltpu.roll(tile, PAIR - half, 1), pltpu.roll(tile, half, 1))
    return tile * cos + partner * sin


def attend_kernel(
    single,
    proj_ref,
    cos_ref,
    sin_ref,
    kv_ref,
    qpos_ref,
    kpos_ref,
    x_ref,
    wo_ref,
    gain_ref,
    query_ref,
    attn_ref,
    lse_ref,
    low_ref,
    residual_ref,
    norm_ref,
    root_ref,
    max_ref,
    sum_ref,
    flat_ref,
):
    chunk = pl.program_id(0)
    rows = x_ref.shape[0]
    width = x_ref.shape[1]

    @pl.when(chunk == 0)
    def _():
        cos, sin = cos_ref[...], sin_ref[...]
        for tile in range((HEADS + 1) // 2):
            turned = turn(proj_ref[:, tile * PAIR : (tile + 1) * PAIR], cos, sin)
            turned = turned.astype(BF16).astype(F32) * HEAD_DIM**-0.5
            for head in range(2 * tile, min(2 * tile + 2, HEADS)):
                at = (head % GROUP) * rows
                placed = place_head(turned, head % 2 == 1, False)
                query_ref[head // GROUP, at : at + rows] = placed.astype(BF16)

    visible = kpos_ref[0] <= qpos_ref[...]
    for g in range(KV_HEADS):
        kv = kv_ref[:, g * PAIR : (g + 1) * PAIR]
        scores = jnp.where(visible, dot_t(query_ref[g], kv), NEG_FILL)
        top = jnp.max(scores, axis=1, keepdims=True)
        if single:
            probs = jnp.exp(scores - top)
            total = jnp.sum(probs, axis=1, keepdims=True)
            attn_ref[g] = matmul(probs.astype(BF16), kv) / total
            lse_ref[g] = top + jnp.log(total)
        else:
            old = jnp.where(chunk == 0, NEG_FILL, max_ref[g])
            top = jnp.maximum(old, top)
            probs = jnp.where(visible, jnp.exp(scores - top), 0.0)
            factor = jnp.where(chunk == 0, 0.0, jnp.exp(old - top))
            sum_ref[g] = jnp.where(chunk == 0, 0.0, factor * sum_ref[g]) + jnp.sum(
                probs, axis=1, keepdims=True
            )
            max_ref[g] = top
            update = matmul(probs.astype(BF16), kv)
            attn_ref[g] = jnp.where(chunk == 0, 0.0, factor * attn_ref[g]) + update

    @pl.when(chunk == pl.num_programs(0) - 1)
    def _():
        if not single:
            for g in range(KV_HEADS):
                attn_ref[g] = attn_ref[g] / sum_ref[g]
                lse_ref[g] = max_ref[g] + jnp.log(sum_ref[g])
        for tile in range((HEADS + 1) // 2):
            both = jnp.zeros((rows, PAIR), F32)
            for head in range(2 * tile, min(2 * tile + 2, HEADS)):
                at = (head % GROUP) * rows
                part = attn_ref[head // GROUP, at : at + rows]
                both = both + place_head(part, True, head % 2 == 1)
            flat_ref[:, tile * PAIR : (tile + 1) * PAIR] = both.astype(BF16)
        low = flat_ref[:, :width]
        low_ref[...] = low
        residual = x_ref[...] + matmul(low, wo_ref[...])
        residual_ref[...] = residual
        root = lax.rsqrt(jnp.mean(residual * residual, axis=1, keepdims=True) + NORM_EPS)
        root_ref[...] = root
        norm_ref[...] = (residual * root * gain_ref[...]).astype(BF16)


def attend_back_kernel(
    grad_ref,
    grad_one_ref,
    grad_two_ref,
    grad_three_ref,
    residual_ref,
    root_ref,
    gain_ref,
    upstream_ref,
    wo_ref,
    query_ref,
    attn_ref,
    lse_ref,
    kv_ref,
    qpos_ref,
    kpos_ref,
    cos_ref,
    sin_ref,
    dx_ref,
    low_ref,
    dgain_ref,
    dq_ref,
    dkv_ref,
    out_grad_ref,
    delta_ref,
    acc_ref,
    flat_ref,
):
    chunk = pl.program_id(0)
    rows = residual_ref.shape[0]
    width = residual_ref.shape[1]

    @pl.when(chunk == 0)
    def _():
        grad = grad_ref[...] + grad_one_ref[...].astype(F32)
        grad = grad + grad_two_ref[...].astype(F32) + grad_three_ref[...].astype(F32)
        residual, root = residual_ref[...], root_ref[...]
        normed = residual * root
        dgain_ref[...] = jnp.sum(grad * normed, axis=0, keepdims=True)
        scaled = gain_ref[...] * grad
        mean = jnp.mean(scaled * residual, axis=1, keepdims=True)
        dx = upstream_ref[...] + root * scaled - residual * (root * root * root) * mean
        dx_ref[...] = dx
        low_ref[...] = dx.astype(BF16)
        flat_ref[:, :width] = dot_t(low_ref[...], wo_ref[...]).astype(BF16).astype(F32)
        for head in range(HEADS):
            at = (head % GROUP) * rows
            tile = flat_ref[:, (head // 2) * PAIR : (head // 2 + 1) * PAIR]
            placed = place_head(tile, head % 2 == 1, True)
            out_grad_ref[head // GROUP, at : at + rows] = placed.astype(BF16)
            attn = attn_ref[head // GROUP, at : at + rows]
            delta_ref[head // GROUP, at : at + rows] = jnp.sum(placed * attn, axis=1, keepdims=True)
        acc_ref[...] = jnp.zeros_like(acc_ref)

    visible = kpos_ref[0] <= qpos_ref[...]
    for g in range(KV_HEADS):
        kv, query, out_grad = kv_ref[:, g * PAIR : (g + 1) * PAIR], query_ref[g], out_grad_ref[g]
        scores = jnp.where(visible, dot_t(query, kv), NEG_FILL)
        probs = jnp.exp(scores - lse_ref[g])
        score_grad = (probs * (dot_t(out_grad, kv) - delta_ref[g])).astype(BF16)
        acc_ref[g] += matmul(score_grad, kv)
        dkv = t_dot(score_grad, query) + t_dot(probs.astype(BF16), out_grad)
        dkv_ref[:, g * PAIR : (g + 1) * PAIR] = dkv.astype(BF16)

    @pl.when(chunk == pl.num_programs(0) - 1)
    def _():
        cos, sin = cos_ref[...], sin_ref[...]
        for tile in range((HEADS + 1) // 2):
            both = jnp.zeros((rows, PAIR), F32)
            for head in range(2 * tile, min(2 * tile + 2, HEADS)):
                at = (head % GROUP) * rows
                part = acc_ref[head // GROUP, at : at + rows]
                both = both + place_head(part, False, head % 2 == 1)
            flat_ref[:, tile * PAIR : (tile + 1) * PAIR] = turn(both, cos, -sin) * HEAD_DIM**-0.5
        dq_ref[...] = flat_ref[:, :width].astype(BF16)


def whole_block(array):
    return pl.BlockSpec(array.shape, lambda c: (0,) * len(array.shape))


def chunk_blocks(pairs, key_pos):
    keys = pairs.shape[0]
    span = min(keys, 1024)
    key_pos = key_pos.reshape(keys // span, 1, span)
    by_keys = pl.BlockSpec((span, pairs.shape[1]), lambda c: (c, 0))
    return keys // span, key_pos, by_keys, pl.BlockSpec((1, 1, span), lambda c: (c, 0, 0))


KERNEL_PARAMS = pltpu.CompilerParams(vmem_limit_bytes=48 * 2**20)


def attend(projected, cos, sin, pairs, query_pos, key_pos, tokens, out_full, gain_row):
    rows, width = tokens.shape
    count, key_pos, by_keys, kpos = chunk_blocks(pairs, key_pos)
    heads = (KV_HEADS, GROUP * rows)
    operands = [projected, cos, sin, pairs, query_pos, key_pos, tokens, out_full, gain_row]
    specs = [whole_block(array) for array in operands]
    specs[3], specs[5] = by_keys, kpos
    shapes = [
        jax.ShapeDtypeStruct(heads + (PAIR,), BF16),
        jax.ShapeDtypeStruct(heads + (PAIR,), F32),
        jax.ShapeDtypeStruct(heads + (1,), F32),
        jax.ShapeDtypeStruct((rows, width), BF16),
        jax.ShapeDtypeStruct((rows, width), F32),
        jax.ShapeDtypeStruct((rows, width), BF16),
        jax.ShapeDtypeStruct((rows, 1), F32),
    ]
    return pl.pallas_call(
        functools.partial(attend_kernel, count == 1),
        grid=(count,),
        in_specs=specs,
        out_specs=[whole_block(shape) for shape in shapes],
        out_shape=shapes,
        scratch_shapes=[
            pltpu.VMEM(heads + (1,), F32),
            pltpu.VMEM(heads + (1,), F32),
            pltpu.VMEM((rows, (HEADS + 1) // 2 * PAIR), BF16),
        ],
        compiler_params=KERNEL_PARAMS,
        name="attend",
    )(*operands)


def attend_back(
    grads, residual, root, gain_row, upstream, out_full, query, attn, lse, pairs, query_pos, key_pos, cos, sin
):
    rows, width = residual.shape
    count, key_pos, by_keys, kpos = chunk_blocks(pairs, key_pos)
    heads = (KV_HEADS, GROUP * rows)
    operands = [*grads, residual, root, gain_row, upstream, out_full, query, attn, lse]
    operands += [pairs, query_pos, key_pos, cos, sin]
    specs = [whole_block(array) for array in operands]
    specs[12], specs[14] = by_keys, kpos
    shapes = [
        jax.ShapeDtypeStruct((rows, width), F32),
        jax.ShapeDtypeStruct((rows, width), BF16),
        jax.ShapeDtypeStruct((1, width), F32),
        jax.ShapeDtypeStruct((rows, HEADS * HEAD_DIM), BF16),
        jax.ShapeDtypeStruct(pairs.shape, BF16),
    ]
    return pl.pallas_call(
        attend_back_kernel,
        grid=(count,),
        in_specs=specs,
        out_specs=[whole_block(shape) for shape in shapes[:4]] + [by_keys],
        out_shape=shapes,
        scratch_shapes=[
            pltpu.VMEM(heads + (PAIR,), BF16),
            pltpu.VMEM(heads + (1,), F32),
            pltpu.VMEM(heads + (PAIR,), F32),
            pltpu.VMEM((rows, (HEADS + 1) // 2 * PAIR), F32),
        ],
        compiler_params=KERNEL_PARAMS,
        name="attend_back",
    )(*operands)


def feed_kernel(*refs):
    norm_refs, cot_refs, (wgu_ref, wd_ref) = refs[:SHARE], refs[SHARE : 2 * SHARE], refs[2 * SHARE : 2 * SHARE + 2]
    grad_refs = refs[2 * SHARE + 2 : 3 * SHARE + 2]
    inner_ref, both_ref, norm_all_ref, cot_all_ref = refs[3 * SHARE + 2 :]
    rows = norm_refs[0].shape[0]
    hidden = wd_ref.shape[0]
    for k in range(SHARE):
        norm_all_ref[k * rows : (k + 1) * rows] = norm_refs[k][...]
        cot_all_ref[k * rows : (k + 1) * rows] = cot_refs[k][...]
    gate_up = matmul(norm_all_ref[...], wgu_ref[...])
    gate, up_part = gate_up[:, :hidden], gate_up[:, hidden:]
    sigma = 1.0 / (1.0 + jnp.exp(-gate))
    activated = gate * sigma
    inner_ref[...] = (activated * up_part).astype(BF16)
    inner_grad = dot_t(cot_all_ref[...], wd_ref[...])
    gate_grad = inner_grad * up_part * sigma * (1.0 + gate * (1.0 - sigma))
    both_ref[:, :hidden] = gate_grad.astype(BF16)
    both_ref[:, hidden:] = (inner_grad * activated).astype(BF16)
    norm_grad = dot_t(both_ref[...], wgu_ref[...])
    for k in range(SHARE):
        grad_refs[k][...] = norm_grad[k * rows : (k + 1) * rows].astype(grad_refs[k].dtype)


def feed(norms, cots, gate_up_own, down_own):
    rows, width = norms[0].shape
    hidden = down_own.shape[0]
    shapes = [jax.ShapeDtypeStruct((rows, width), BF16 if k else F32) for k in range(SHARE)]
    shapes += [
        jax.ShapeDtypeStruct((SHARE * rows, hidden), BF16),
        jax.ShapeDtypeStruct((SHARE * rows, 2 * hidden), BF16),
        jax.ShapeDtypeStruct((SHARE * rows, width), BF16),
        jax.ShapeDtypeStruct((SHARE * rows, width), BF16),
    ]
    out = pl.pallas_call(
        feed_kernel,
        out_shape=shapes,
        compiler_params=KERNEL_PARAMS,
        name="feed",
    )(*norms, *cots, gate_up_own, down_own)
    return out[:SHARE], *out[SHARE:]


def feed_out_kernel(inner_ref, wd_ref, *out_refs):
    rows = out_refs[0].shape[0]
    out = matmul(inner_ref[...], wd_ref[...])
    for k in range(SHARE):
        out_refs[k][...] = out[k * rows : (k + 1) * rows].astype(out_refs[k].dtype)


def feed_out(inner_low, down_own):
    rows, width = inner_low.shape[0] // SHARE, down_own.shape[1]
    return pl.pallas_call(
        feed_out_kernel,
        out_shape=[jax.ShapeDtypeStruct((rows, width), BF16 if k else F32) for k in range(SHARE)],
        compiler_params=KERNEL_PARAMS,
        name="feed_out",
    )(inner_low, down_own)


def rotation(positions):
    half_len = HEAD_DIM // 2
    freq_table = THETA ** (-jnp.arange(half_len, dtype=F32) / half_len)
    angle_table = positions.astype(F32)[:, None] * freq_table[None, :]
    return (jnp.cos(angle_table)[:, None, :], jnp.sin(angle_table)[:, None, :])


def rotate(values, cos_table, sin_table):
    half_len = values.shape[-1] // 2
    leading = values[..., :half_len]
    trailing = values[..., half_len:]
    return jnp.concatenate(
        [leading * cos_table - trailing * sin_table, trailing * cos_table + leading * sin_table],
        axis=-1,
    )


def rotate_back(values, cos_table, sin_table):
    return rotate(values, cos_table, -sin_table)


def rms_forward(values, gain_row):
    inv_root = lax.rsqrt(jnp.mean(values * values, axis=-1, keepdims=True) + NORM_EPS)
    return (values * inv_root * gain_row, inv_root)


def rms_backward(values, inv_root, gain_row, grad_out):
    scaled = gain_row * grad_out
    return inv_root * scaled - values * inv_root**3 * jnp.mean(
        scaled * values, axis=-1, keepdims=True
    )


def adamw(weight, moment_one, moment_two, gradient, step_rate, decay_rate):
    first_new = BETA_ONE * moment_one + (1.0 - BETA_ONE) * gradient
    second_new = BETA_TWO * moment_two + (1.0 - BETA_TWO) * gradient * gradient
    first_hat = first_new / (1.0 - BETA_ONE**STEP)
    second_hat = second_new / (1.0 - BETA_TWO**STEP)
    weight_new = weight - step_rate * (
        first_hat / (jnp.sqrt(second_hat) + ADAM_EPS) + decay_rate * weight
    )
    return (weight_new, first_new, second_new)


def own_columns(array, ctx_rank, ctx_count):
    col_width = array.shape[1] // ctx_count
    return lax.dynamic_slice_in_dim(array, ctx_rank * col_width, col_width, 1)


def local(
    layer_input,
    cotangent,
    block_order,
    qkv_weight,
    qkv_first,
    qkv_second,
    out_weight,
    out_first,
    out_second,
    gate_up_weight,
    gate_up_first,
    gate_up_second,
    down_weight,
    down_first,
    down_second,
    gains,
    gain_first,
    gain_second,
):
    ctx_rank = lax.axis_index("ctx")
    ctx_count = lax.axis_size("ctx")
    wa_rank = lax.axis_index("wa")
    wa_count = lax.axis_size("wa")
    place = ctx_rank % SHARE
    tokens = layer_input[0]
    upstream = cotangent[0]
    tok_rows, width = tokens.shape
    shard = width // wa_count
    hidden = FF // SHARE
    query_width = HEADS * HEAD_DIM
    pair_width = KV_HEADS * HEAD_DIM
    half_len = tok_rows // 2

    qkv_low = qkv_weight.astype(BF16)
    qkv_blocks = gather_relative(qkv_low, "wa")
    gains_low = gains.astype(BF16)
    gain_blocks = [gains_low] + [flip(gains_low, "wa", k) for k in range(1, wa_count)]
    gain_norm = in_order([block[None] for block in gain_blocks], "wa").astype(F32)
    gain_norm = gain_norm.transpose(1, 0, 2).reshape(2, width)
    cot_low = upstream.astype(BF16)
    cots = share_gather(cot_low)
    qkv_full = in_order(qkv_blocks, "wa")

    arrived = qkv_blocks[wa_count // 2]
    out_late, gate_up_late, down_late, arrived = lax.optimization_barrier(
        (out_weight, gate_up_weight, down_weight, arrived)
    )
    out_full = lax.all_gather(out_late.astype(BF16), "wa", axis=0, tiled=True)
    gate_up_part = jnp.concatenate(
        [
            lax.dynamic_slice_in_dim(gate_up_late, place * hidden, hidden, 1),
            lax.dynamic_slice_in_dim(gate_up_late, FF + place * hidden, hidden, 1),
        ],
        axis=1,
    )
    gate_up_own = lax.all_gather(gate_up_part.astype(BF16), "wa", axis=0, tiled=True)
    down_rows = FF // wa_count // SHARE
    down_piece = lax.dynamic_slice_in_dim(down_late, place * down_rows, down_rows, 0)
    down_own = lax.all_gather(swap_places(down_piece.astype(BF16)), "wa", axis=0, tiled=True)

    ring = jnp.array(ring_order(ctx_count), jnp.int32)
    ring_place = jnp.argsort(ring).astype(jnp.int32)[ctx_rank]
    order = block_order[0].reshape(ctx_count, 2)
    offsets = jnp.arange(half_len, dtype=jnp.int32)
    key_starts = order[ring[(ring_place + jnp.arange(ctx_count)) % ctx_count]]
    key_pos = (key_starts[:, :, None] * half_len + offsets).reshape(-1)
    own_pos = key_pos[:tok_rows]
    query_pos = jnp.tile(own_pos, GROUP)[:, None]
    cos_table, sin_table = rotation(own_pos)
    cos_lanes = jnp.tile(cos_table[:, 0], (1, 4))
    sin_lanes = jnp.tile(jnp.concatenate([-sin_table[:, 0], sin_table[:, 0]], axis=1), (1, 2))

    norm_one, root_one = rms_forward(tokens, gain_norm[0])
    norm_one_low = norm_one.astype(BF16)
    projected = matmul(norm_one_low, qkv_full)
    keys = rotate(
        projected[:, query_width : query_width + pair_width].reshape(tok_rows, KV_HEADS, HEAD_DIM),
        cos_table,
        sin_table,
    )
    values = projected[:, query_width + pair_width :].reshape(tok_rows, KV_HEADS, HEAD_DIM)
    pair_low = jnp.concatenate([keys, values], axis=-1).astype(BF16)
    pairs = jnp.concatenate(ring_gather(pair_low.reshape(tok_rows, KV_HEADS * PAIR)))
    padded = (HEADS + 1) // 2 * PAIR - query_width
    query_proj = jnp.pad(projected[:, :query_width], ((0, 0), (0, padded)))

    query_low, attn, log_total, attn_low, residual, norm_two_low, root_two = attend(
        query_proj, cos_lanes, sin_lanes, pairs, query_pos, key_pos, tokens, out_full, gain_norm[1:2]
    )

    norms = share_gather(norm_two_low)
    grads, inner_low, gate_up_grad_low, norm_two_all, cot_all = feed(
        norms, cots, gate_up_own, down_own
    )
    grads = [grads[0]] + share_send(grads[1:])
    outs = feed_out(inner_low, down_own)
    outs = [outs[0]] + share_send(outs[1:])
    layer_output = residual + sum(part.astype(F32) for part in outs)

    gate_up_sum = t_dot(norm_two_all, gate_up_grad_low).astype(BF16)
    gate_up_sum = gate_up_sum.reshape(wa_count, shard, 2 * hidden)
    gate_up_sum = scatter_sum(gate_up_sum, 0, "wa")
    high_bits = bits_of(ctx_count, SHARE)
    groups = ctx_count // SHARE
    part_cols = 2 * FF // ctx_count
    gate_up_sum = gate_up_sum.reshape(shard, groups, part_cols).transpose(1, 0, 2)
    gate_up_sum = scatter_sum(gate_up_sum, 0, "ctx", high_bits)
    moves = []
    for ctx in range(ctx_count):
        high, low = ctx // SHARE, ctx % SHARE
        per_half = groups // 2
        moves.append((ctx, ((high // per_half) * SHARE + low) * per_half + high % per_half))
    if any(source != target for source, target in moves):
        gate_up_sum = lax.ppermute(gate_up_sum, "ctx", moves)
    gate_up_sum = gate_up_sum.astype(F32)
    down_sum = t_dot(cot_all, inner_low).astype(BF16)
    down_sum = down_sum.reshape(groups, wa_count, width // ctx_count, hidden)
    down_sum = scatter_sum(down_sum, 1, "wa")
    down_sum = scatter_sum(down_sum, 0, "ctx", high_bits)
    down_sum = swap_places(down_sum).astype(F32).T

    residual_grad, res_low, gain_two_grad, query_pre, pair_grad = attend_back(
        grads,
        residual,
        root_two,
        gain_norm[1:2],
        upstream,
        out_full,
        query_low,
        attn,
        log_total,
        pairs,
        query_pos,
        key_pos,
        cos_lanes,
        sin_lanes,
    )
    pair_sum = ring_reduce(lambda k: pair_grad[k * tok_rows : (k + 1) * tok_rows])
    pair_sum = pair_sum.reshape(tok_rows, KV_HEADS, PAIR)
    key_pre = rotate_back(pair_sum[:, :, :HEAD_DIM], cos_table, sin_table)
    projected_grad_low = jnp.concatenate(
        [
            query_pre,
            key_pre.reshape(tok_rows, pair_width).astype(BF16),
            pair_sum[:, :, HEAD_DIM:].reshape(tok_rows, pair_width).astype(BF16),
        ],
        axis=1,
    )
    norm_one_grad = dot_t(projected_grad_low, qkv_full)
    input_grad = residual_grad + rms_backward(tokens, root_one, gain_norm[0], norm_one_grad)

    out_cols = width // ctx_count
    out_parts = jnp.einsum(
        "td,tnc->ndc",
        attn_low,
        res_low.reshape(tok_rows, ctx_count, out_cols),
        preferred_element_type=F32,
    )
    gain_column = jnp.broadcast_to(gain_two_grad.reshape(1, width, 1), (ctx_count, width, 1))
    out_parts = jnp.concatenate([out_parts, gain_column], axis=2).astype(BF16)
    out_parts = out_parts.reshape(ctx_count, wa_count, shard, out_cols + 1)
    out_parts = scatter_sum(scatter_sum(out_parts, 1, "wa"), 0, "ctx").astype(F32)
    out_sum, gain_two_sum = out_parts[:, :out_cols], out_parts[:, out_cols]

    qkv_cols = qkv_weight.shape[1] // ctx_count
    norm_shards = norm_one_low.reshape(tok_rows, wa_count, shard)
    norm_rows = jnp.concatenate(
        [
            flip(lax.dynamic_index_in_dim(norm_shards, wa_rank ^ k, 1, keepdims=False), "wa", k)
            if k
            else lax.dynamic_index_in_dim(norm_shards, wa_rank, 1, keepdims=False)
            for k in range(wa_count)
        ]
    )
    grad_rows = jnp.concatenate(gather_relative(projected_grad_low, "wa"))
    qkv_parts = jnp.einsum(
        "td,tnc->ndc",
        norm_rows,
        grad_rows.reshape(wa_count * tok_rows, ctx_count, qkv_cols),
        preferred_element_type=F32,
    )
    weight_parts = qkv_low.reshape(shard, ctx_count, qkv_cols).transpose(1, 0, 2).astype(F32)
    gain_one_rows = jnp.sum(qkv_parts * weight_parts, axis=(0, 2))
    own_gain = gains[0].astype(BF16).astype(F32)
    gain_column = jnp.broadcast_to((gain_one_rows / own_gain)[None, :, None], (ctx_count, shard, 1))
    qkv_parts = jnp.concatenate([qkv_parts, gain_column], axis=2).astype(BF16)
    qkv_parts = scatter_sum(qkv_parts, 0, "ctx").astype(F32)
    qkv_sum, gain_one_sum = qkv_parts[:, :qkv_cols], qkv_parts[:, qkv_cols]
    gain_sum = jnp.stack([gain_one_sum, gain_two_sum])

    updates = []
    for weight, first, second, gradient in (
        (qkv_weight, qkv_first, qkv_second, qkv_sum),
        (out_weight, out_first, out_second, out_sum),
        (gate_up_weight, gate_up_first, gate_up_second, gate_up_sum),
        (down_weight, down_first, down_second, down_sum),
    ):
        slices = [own_columns(array, ctx_rank, ctx_count) for array in (weight, first, second)]
        updates += adamw(*slices, gradient, RATE_MATRIX, WEIGHT_DECAY)
    updates += adamw(gains, gain_first, gain_second, gain_sum, RATE_GAIN, 0.0)
    return (
        layer_output[None],
        input_grad[None],
        *updates,
        qkv_sum,
        out_sum,
        gate_up_sum,
        down_sum,
        gain_sum,
    )


def solution(mesh):
    rows = P("wa", None)
    tokens = P("wa", "ctx", None)
    piece = P("wa", "ctx")
    gain = P(None, "wa")
    return jax.shard_map(
        local,
        mesh=mesh,
        in_specs=(tokens, tokens) + (rows,) * 13 + (gain,) * 3,
        out_specs=(tokens, tokens) + (piece,) * 12 + (gain,) * 3 + (piece,) * 4 + (gain,),
        check_vma=False,
    )
```

```python
import functools

import jax
import jax.numpy as jnp
from jax import lax
from jax.experimental import pallas as pl
from jax.experimental.pallas import tpu as pltpu
from jax.sharding import PartitionSpec as P

HEADS = 15
KV_HEADS = 5
GROUP = HEADS // KV_HEADS
HEAD_DIM = 64
PAIR = 2 * HEAD_DIM
FF = 2560
STEP = 10
SHARE = 4

NEG_FILL = -1e30
NORM_EPS = 1e-05
THETA = 10000.0
BETA_ONE = 0.9
BETA_TWO = 0.999
ADAM_EPS = 1e-08
RATE_MATRIX = 0.05
RATE_GAIN = 0.5
WEIGHT_DECAY = 0.1
BF16 = jnp.bfloat16
F32 = jnp.float32


def matmul(left, right):
    return jnp.dot(left, right, preferred_element_type=F32)


def flip(value, axis, bit):
    count = lax.axis_size(axis)
    return lax.ppermute(value, axis, [(i, i ^ bit) for i in range(count)])


def bits_of(count, first=1):
    bits = []
    while first < count:
        bits.append(first)
        first *= 2
    return bits


def gather_relative(value, axis):
    blocks = {0: value}
    for bit in reversed(bits_of(lax.axis_size(axis))):
        blocks.update({key | bit: flip(block, axis, bit) for key, block in blocks.items()})
    return [blocks[key] for key in sorted(blocks)]


def in_order(blocks, axis):
    rank = lax.axis_index(axis)
    rows = blocks[0].shape[0]
    whole = jnp.zeros((len(blocks) * rows,) + blocks[0].shape[1:], blocks[0].dtype)
    for key, block in enumerate(blocks):
        whole = lax.dynamic_update_slice_in_dim(whole, block, (rank ^ key) * rows, 0)
    return whole


def halve(pieces, dim, axis, bits, place):
    rank = lax.axis_index(axis)
    for bit, part_bit in zip(bits, place):
        shape = pieces.shape
        low = part_bit
        high = shape[dim] // (2 * low)
        split = pieces.reshape(shape[:dim] + (high, 2, low) + shape[dim + 1 :])
        side = ((rank & bit) != 0).astype(jnp.int32)
        mine = lax.dynamic_index_in_dim(split, side, dim + 1, keepdims=False)
        other = lax.dynamic_index_in_dim(split, 1 - side, dim + 1, keepdims=False)
        got = flip(other, axis, bit)
        pieces = (mine.astype(F32) + got.astype(F32)).astype(BF16)
        pieces = pieces.reshape(shape[:dim] + (high * low,) + shape[dim + 1 :])
    return pieces


def scatter_sum(pieces, dim, axis, bits=None):
    count = lax.axis_size(axis)
    bits = bits_of(count) if bits is None else bits
    return halve(pieces, dim, axis, bits, [1] * len(bits)).squeeze(dim)


def send_place(index):
    return lambda count: (index % 2) * (count // 2) + index // 2


def pieces_parts(pieces, axis):
    count = pieces.shape[0]
    keep, send = pieces[: count // 2], pieces[count // 2 :]
    pieces = keep.astype(F32) + flip(send, axis, 1).astype(F32)
    low = pieces.astype(BF16)
    return low, [pieces[0]] + [flip(low[j], axis, 2 * j) for j in range(1, count // 2)]


def far_bits():
    return bits_of(lax.axis_size("ctx"), SHARE)


def pair_offsets():
    high = [0]
    for bit in far_bits():
        high += [r | bit for r in high]
    return [k | r for k in range(SHARE) for r in high]


def pair_gather(block):
    blocks = [block]
    for bit in far_bits():
        blocks += [flip(other, "ctx", bit) for other in blocks]
    rows = list(blocks)
    for k in range(1, SHARE):
        rows += [flip(other, "ctx", k) for other in blocks]
    return jnp.concatenate(rows)


def pair_reduce(parts, beside):
    got = [flip(part, "ctx", k + 1) for k, part in enumerate(parts[1:])]
    got, beside = lax.optimization_barrier((got, beside))
    total = sum(part.astype(F32) for part in [parts[0], *got])
    terms = [total]
    for bit in reversed(far_bits()):
        total = sum(term.astype(F32) for term in terms)
        half = total.shape[0] // 2
        terms = [total[:half], flip(total[half:].astype(BF16), "ctx", bit)]
    return beside, terms


def share_gather(block):
    return [block] + [flip(block, "ctx", k) for k in range(1, SHARE)]


def share_send(parts):
    return [flip(part, "ctx", k + 1) for k, part in enumerate(parts)]


def swap_places(value):
    count, shards = lax.axis_size("ctx"), lax.axis_size("wa")
    pairs = []
    for ctx in range(count):
        for own in range(shards):
            high, low = ctx // SHARE, ctx % SHARE
            pairs.append((ctx * shards + own, (high * SHARE + own) * shards + low))
    return lax.ppermute(value, ("ctx", "wa"), pairs)


def dot_t(left, right):
    return lax.dot_general(left, right, (((1,), (1,)), ((), ())), preferred_element_type=F32)


def t_dot(left, right):
    return lax.dot_general(left, right, (((0,), (0,)), ((), ())), preferred_element_type=F32)


def lanes(rows):
    return lax.broadcasted_iota(jnp.int32, (rows, PAIR), 1)


def place_head(tile, odd, upper):
    if odd != upper:
        tile = pltpu.roll(tile, HEAD_DIM, 1)
    half = lanes(tile.shape[0]) >= HEAD_DIM
    return jnp.where(half if upper else jnp.logical_not(half), tile, 0.0)


def query_positions(starts_ref, rows):
    half = rows // 2
    row = lax.broadcasted_iota(jnp.int32, (GROUP * rows, 1), 0) % rows
    start = jnp.where(row < half, starts_ref[0], starts_ref[1] - 1)
    return start * half + row


def turn(tile, cos, sin):
    half = HEAD_DIM // 2
    leading = (lanes(tile.shape[0]) % HEAD_DIM) < half
    partner = jnp.where(leading, pltpu.roll(tile, PAIR - half, 1), pltpu.roll(tile, half, 1))
    return tile * cos + partner * sin


def pack_kernel(weight_ref, gain_ref, out_ref):
    columns = weight_ref.shape[1]
    out_ref[:, :columns] = weight_ref[...].astype(BF16)
    eye = lax.broadcasted_iota(jnp.int32, (2, 2), 0) == lax.broadcasted_iota(jnp.int32, (2, 2), 1)
    turned = t_dot(gain_ref[...].astype(BF16).astype(F32), jnp.where(eye, 1.0, 0.0))
    out_ref[:, columns:] = turned.astype(BF16)


def pack(weight, gains):
    rows, columns = weight.shape
    return pl.pallas_call(
        pack_kernel,
        out_shape=jax.ShapeDtypeStruct((rows, columns + 2), BF16),
        compiler_params=KERNEL_PARAMS,
        cost_estimate=cost(1.5),
        name="pack",
    )(weight, gains)


def project_kernel(
    rank_ref, x_ref, cos_ref, sin_ref, *refs
):
    blocks = refs[:-9]
    query_ref, pair_ref, cols_ref, root_ref, gain_ref = refs[-9:-4]
    full_ref, norm_ref, flat_ref, turned_ref = refs[-4:]
    rank = rank_ref[0]
    rows, width = x_ref.shape
    shard, columns = blocks[0].shape
    columns -= 2
    eye = lax.broadcasted_iota(jnp.int32, (shard, shard), 0) == lax.broadcasted_iota(
        jnp.int32, (shard, shard), 1
    )
    eye = jnp.where(eye, 1.0, 0.0).astype(BF16)
    for k, block in enumerate(blocks):
        at = pl.ds(pl.multiple_of((rank ^ k) * shard, 16), shard)
        full_ref[at, :] = block[:, :columns]
        turned_ref[rank ^ k] = t_dot(block[:, columns:], eye)
    for j in range(len(blocks)):
        gain_ref[:, j * shard : (j + 1) * shard] = turned_ref[j]
    x = x_ref[...]
    root = lax.rsqrt(jnp.mean(x * x, axis=1, keepdims=True) + NORM_EPS)
    root_ref[...] = root
    norm_ref[...] = x * root * gain_ref[0:1]
    for j in range(len(blocks)):
        cols_ref[rank ^ j] = norm_ref[:, j * shard : (j + 1) * shard].astype(BF16)
    flat_ref[:, :columns] = matmul(norm_ref[...].astype(BF16), full_ref[...])
    cos, sin = cos_ref[...], sin_ref[...]

    def tile_of(head):
        at = head // 2 * PAIR
        return flat_ref[:, at : at + PAIR]

    for g in range(KV_HEADS):
        key, value = HEADS + g, HEADS + KV_HEADS + g
        both = place_head(turn(tile_of(key), cos, sin), key % 2 == 1, False)
        both = both + place_head(tile_of(value), value % 2 == 1, True)
        pair_ref[:, g * PAIR : (g + 1) * PAIR] = both.astype(BF16)
    for head in range(HEADS):
        at = (head % GROUP) * rows
        placed = place_head(turn(tile_of(head), cos, sin), head % 2 == 1, False)
        placed = placed.astype(BF16).astype(F32) * HEAD_DIM**-0.5
        query_ref[head // GROUP, at : at + rows] = placed.astype(BF16)


def project(rank, tokens, cos, sin, blocks):
    rows, width = tokens.shape
    shard, columns = blocks[0].shape
    columns -= 2
    units = HEADS + 2 * KV_HEADS
    vmem = pl.BlockSpec(memory_space=pltpu.VMEM)
    shapes = [
        far_out((KV_HEADS, GROUP * rows, PAIR), BF16),
        far_out((rows, KV_HEADS * PAIR), BF16),
        far_out((len(blocks), rows, shard), BF16),
        far_out((rows, 1), F32),
        far_out((2, width), F32),
        far_out((width, columns), BF16),
    ]
    return pl.pallas_call(
        project_kernel,
        in_specs=[pl.BlockSpec(memory_space=pltpu.SMEM)] + [vmem] * (3 + len(blocks)),
        out_specs=[vmem] * len(shapes),
        out_shape=shapes,
        scratch_shapes=[
            pltpu.VMEM((rows, width), F32),
            pltpu.VMEM((rows, (units + 1) // 2 * PAIR), F32),
            pltpu.VMEM((len(blocks), 2, shard), F32),
        ],
        compiler_params=KERNEL_PARAMS,
        cost_estimate=cost(4.5),
        name="project",
    )(rank, tokens, cos, sin, *blocks)


def attend_kernel(
    single,
    query_ref,
    kv_ref,
    starts_ref,
    kpos_ref,
    x_ref,
    gain_ref,
    wo_ref,
    attn_ref,
    lse_ref,
    low_ref,
    residual_ref,
    norm_ref,
    root_ref,
    max_ref,
    sum_ref,
    flat_ref,
):
    chunk = pl.program_id(0)
    rows = x_ref.shape[0]
    width = x_ref.shape[1]

    visible = kpos_ref[0] <= query_positions(starts_ref, rows)
    for g in range(KV_HEADS):
        kv = kv_ref[:, g * PAIR : (g + 1) * PAIR]
        scores = jnp.where(visible, dot_t(query_ref[g], kv), NEG_FILL)
        top = jnp.max(scores, axis=1, keepdims=True)
        if single:
            probs = jnp.exp(scores - top)
            total = jnp.sum(probs, axis=1, keepdims=True)
            attn_ref[g] = matmul(probs.astype(BF16), kv) / total
            lse_ref[g] = top + jnp.log(total)
        else:
            old = jnp.where(chunk == 0, NEG_FILL, max_ref[g])
            top = jnp.maximum(old, top)
            probs = jnp.where(visible, jnp.exp(scores - top), 0.0)
            factor = jnp.where(chunk == 0, 0.0, jnp.exp(old - top))
            sum_ref[g] = jnp.where(chunk == 0, 0.0, factor * sum_ref[g]) + jnp.sum(
                probs, axis=1, keepdims=True
            )
            max_ref[g] = top
            update = matmul(probs.astype(BF16), kv)
            attn_ref[g] = jnp.where(chunk == 0, 0.0, factor * attn_ref[g]) + update

    @pl.when(chunk == pl.num_programs(0) - 1)
    def _():
        if not single:
            for g in range(KV_HEADS):
                attn_ref[g] = attn_ref[g] / sum_ref[g]
                lse_ref[g] = max_ref[g] + jnp.log(sum_ref[g])
        for tile in range((HEADS + 1) // 2):
            both = jnp.zeros((rows, PAIR), F32)
            for head in range(2 * tile, min(2 * tile + 2, HEADS)):
                at = (head % GROUP) * rows
                part = attn_ref[head // GROUP, at : at + rows]
                both = both + place_head(part, True, head % 2 == 1)
            flat_ref[:, tile * PAIR : (tile + 1) * PAIR] = both.astype(BF16)
        low = flat_ref[:, :width]
        low_ref[...] = low
        residual = x_ref[...] + matmul(low, wo_ref[:, -width:])
        residual_ref[...] = residual
        root = lax.rsqrt(jnp.mean(residual * residual, axis=1, keepdims=True) + NORM_EPS)
        root_ref[...] = root
        norm_ref[...] = (residual * root * gain_ref[1:2]).astype(BF16)


def attend_back_kernel(
    grad_ref,
    grad_one_ref,
    grad_two_ref,
    grad_three_ref,
    residual_ref,
    root_ref,
    gain_ref,
    upstream_ref,
    wo_ref,
    query_ref,
    attn_ref,
    lse_ref,
    kv_ref,
    starts_ref,
    kpos_ref,
    cos_ref,
    sin_ref,
    *refs,
):
    dx_ref, low_ref, dq_ref, dgain_ref = refs[:4]
    dkv_refs = refs[4:-4]
    out_grad_ref, delta_ref, acc_ref, flat_ref = refs[-4:]
    chunk = pl.program_id(0)
    rows = residual_ref.shape[0]
    width = residual_ref.shape[1]

    @pl.when(chunk == 0)
    def _():
        grad = grad_ref[...] + grad_one_ref[...].astype(F32)
        grad = grad + grad_two_ref[...].astype(F32) + grad_three_ref[...].astype(F32)
        residual, root = residual_ref[...], root_ref[...]
        dgain_ref[...] = (grad * residual * root).astype(BF16)
        scaled = gain_ref[1:2] * grad
        mean = jnp.mean(scaled * residual, axis=1, keepdims=True)
        dx = upstream_ref[...] + root * scaled - residual * (root * root * root) * mean
        dx_ref[...] = dx
        low_ref[...] = dx.astype(BF16)
        flat_ref[:, :width] = dot_t(low_ref[...], wo_ref[:, -width:]).astype(BF16).astype(F32)
        for head in range(HEADS):
            at = (head % GROUP) * rows
            tile = flat_ref[:, (head // 2) * PAIR : (head // 2 + 1) * PAIR]
            placed = place_head(tile, head % 2 == 1, True)
            out_grad_ref[head // GROUP, at : at + rows] = placed.astype(BF16)
            attn = attn_ref[head // GROUP, at : at + rows]
            delta_ref[head // GROUP, at : at + rows] = jnp.sum(placed * attn, axis=1, keepdims=True)
        acc_ref[...] = jnp.zeros_like(acc_ref)

    visible = kpos_ref[0] <= query_positions(starts_ref, rows)
    for g in range(KV_HEADS):
        kv, query, out_grad = kv_ref[:, g * PAIR : (g + 1) * PAIR], query_ref[g], out_grad_ref[g]
        scores = jnp.where(visible, dot_t(query, kv), NEG_FILL)
        probs = jnp.exp(scores - lse_ref[g])
        score_grad = (probs * (dot_t(out_grad, kv) - delta_ref[g])).astype(BF16)
        acc_ref[g] += matmul(score_grad, kv)
        dkv = t_dot(score_grad, query) + t_dot(probs.astype(BF16), out_grad)
        span = dkv_refs[0].shape[0]
        for index, dkv_ref in enumerate(dkv_refs):
            part = dkv[index * span : (index + 1) * span]
            dkv_ref[:, g * PAIR : (g + 1) * PAIR] = part.astype(BF16)

    @pl.when(chunk == pl.num_programs(0) - 1)
    def _():
        cos, sin = cos_ref[...], sin_ref[...]
        for tile in range((HEADS + 1) // 2):
            both = jnp.zeros((rows, PAIR), F32)
            for head in range(2 * tile, min(2 * tile + 2, HEADS)):
                at = (head % GROUP) * rows
                part = acc_ref[head // GROUP, at : at + rows]
                both = both + place_head(part, False, head % 2 == 1)
            flat_ref[:, tile * PAIR : (tile + 1) * PAIR] = turn(both, cos, -sin) * HEAD_DIM**-0.5
        dq_ref[...] = flat_ref[:, :width].astype(BF16)


def whole_block(array):
    return pl.BlockSpec(array.shape, lambda c: (0,) * len(array.shape))


def chunk_blocks(pairs, key_pos):
    keys = pairs.shape[0]
    span = min(keys, 1024)
    key_pos = key_pos.reshape(keys // span, 1, span)
    by_keys = pl.BlockSpec((span, pairs.shape[1]), lambda c: (c, 0))
    return keys // span, key_pos, by_keys, pl.BlockSpec((1, 1, span), lambda c: (c, 0, 0))


KERNEL_PARAMS = pltpu.CompilerParams(vmem_limit_bytes=60 * 2**20)


def cost(micros):
    return pl.CostEstimate(flops=0, bytes_accessed=int(micros * 3.0e6), transcendentals=0)


def far_out(shape, dtype):
    return pltpu.HBM(shape, dtype)


def assemble(rank, blocks, whole_ref):
    shard = blocks[0].shape[0]
    for k, block in enumerate(blocks):
        whole_ref[pl.ds(pl.multiple_of((rank ^ k) * shard, 16), shard), :] = block[...]


def attend(query, pairs, starts, key_pos, tokens, gain_row, out_full):
    rows, width = tokens.shape
    count, key_pos, by_keys, kpos = chunk_blocks(pairs, key_pos)
    heads = (KV_HEADS, GROUP * rows)
    operands = [query, pairs, starts, key_pos, tokens, gain_row, out_full]
    specs = [whole_block(array) for array in operands]
    specs[1], specs[2], specs[3] = by_keys, pl.BlockSpec(memory_space=pltpu.SMEM), kpos
    shapes = [
        far_out(heads + (PAIR,), F32),
        far_out(heads + (1,), F32),
        far_out((rows, width), BF16),
        far_out((rows, width), F32),
        far_out((rows, width), BF16),
        far_out((rows, 1), F32),
    ]
    return pl.pallas_call(
        functools.partial(attend_kernel, count == 1),
        grid=(count,),
        in_specs=specs,
        out_specs=[whole_block(shape) for shape in shapes],
        out_shape=shapes,
        scratch_shapes=[
            pltpu.VMEM(heads + (1,), F32),
            pltpu.VMEM(heads + (1,), F32),
            pltpu.VMEM((rows, (HEADS + 1) // 2 * PAIR), BF16),
        ],
        compiler_params=KERNEL_PARAMS,
        cost_estimate=cost(6.5),
        name="attend",
    )(*operands)


def attend_back(
    grads,
    residual,
    root,
    gain_row,
    upstream,
    out_full,
    query,
    attn,
    lse,
    pairs,
    starts,
    key_pos,
    cos,
    sin,
):
    rows, width = residual.shape
    count, key_pos, by_keys, kpos = chunk_blocks(pairs, key_pos)
    heads = (KV_HEADS, GROUP * rows)
    operands = [*grads, residual, root, gain_row, upstream, out_full, query, attn, lse]
    operands += [pairs, starts, key_pos, cos, sin]
    specs = [whole_block(array) for array in operands]
    specs[12], specs[13], specs[14] = by_keys, pl.BlockSpec(memory_space=pltpu.SMEM), kpos
    span = pairs.shape[0] // SHARE
    shapes = [
        far_out((rows, width), F32),
        far_out((rows, width), BF16),
        far_out((rows, HEADS * HEAD_DIM), BF16),
        far_out((rows, width), BF16),
    ]
    out_specs = [whole_block(shape) for shape in shapes]
    if count == 1:
        shapes += [far_out((span, pairs.shape[1]), BF16)] * SHARE
        out_specs += [whole_block(shapes[-1])] * SHARE
    else:
        shapes.append(jax.ShapeDtypeStruct(pairs.shape, BF16))
        out_specs.append(by_keys)
    out = pl.pallas_call(
        attend_back_kernel,
        grid=(count,),
        in_specs=specs,
        out_specs=out_specs,
        out_shape=shapes,
        scratch_shapes=[
            pltpu.VMEM(heads + (PAIR,), BF16),
            pltpu.VMEM(heads + (1,), F32),
            pltpu.VMEM(heads + (PAIR,), F32),
            pltpu.VMEM((rows, (HEADS + 1) // 2 * PAIR), F32),
        ],
        compiler_params=KERNEL_PARAMS,
        cost_estimate=cost(10),
        name="attend_back",
    )(*operands)
    parts = out[4:]
    if count > 1:
        parts = [parts[0][k * span : (k + 1) * span] for k in range(SHARE)]
    return *out[:4], parts


def join_kernel(dq_ref, cos_ref, sin_ref, *refs):
    parts, (out_ref, flat_ref) = refs[:-2], refs[-2:]
    columns = out_ref.shape[1]
    cos, sin = cos_ref[...], sin_ref[...]
    flat_ref[...] = jnp.zeros_like(flat_ref)
    flat_ref[:, : dq_ref.shape[1]] = dq_ref[...].astype(F32)
    for g in range(KV_HEADS):
        key, value = HEADS + g, HEADS + KV_HEADS + g
        total = parts[0][:, g * PAIR : (g + 1) * PAIR].astype(F32)
        for part in parts[1:]:
            total = total + part[:, g * PAIR : (g + 1) * PAIR].astype(F32)
        at = key // 2 * PAIR
        flat_ref[:, at : at + PAIR] += place_head(turn(total, cos, -sin), False, key % 2 == 1)
        at = value // 2 * PAIR
        flat_ref[:, at : at + PAIR] += place_head(total, True, value % 2 == 1)
    out_ref[...] = flat_ref[:, :columns].astype(BF16)


def join(query_grad, cos, sin, parts):
    rows = query_grad.shape[0]
    units = HEADS + 2 * KV_HEADS
    return pl.pallas_call(
        join_kernel,
        out_shape=jax.ShapeDtypeStruct((rows, units * HEAD_DIM), BF16),
        scratch_shapes=[pltpu.VMEM((rows, (units + 1) // 2 * PAIR), F32)],
        compiler_params=KERNEL_PARAMS,
        cost_estimate=cost(1.6),
        name="join",
    )(query_grad, cos, sin, *parts)


def out_grad_kernel(rank_ref, attn_ref, grad_ref, gain_ref, out_ref, flat_ref):
    shards, count, shard, columns = out_ref.shape
    columns -= 1
    ones = jnp.ones((gain_ref.shape[0], PAIR), BF16)
    gain = t_dot(gain_ref[...], ones)[:, :1].astype(BF16)
    flat_ref[...] = t_dot(attn_ref[...], grad_ref[...])
    for n in range(count):
        for j in range(shards):
            part = flat_ref[j * shard : (j + 1) * shard, n * columns : (n + 1) * columns]
            row, col = send_place(rank_ref[0] ^ j)(shards), send_place(rank_ref[1] ^ n)(count)
            out_ref[row, col, :, :columns] = part.astype(BF16)
            out_ref[row, col, :, columns:] = gain[j * shard : (j + 1) * shard]


def out_gradient(ranks, attn_low, res_low, gain_terms, shards, count):
    rows, width = attn_low.shape
    shape = (shards, count, width // shards, res_low.shape[1] // count + 1)
    vmem = pl.BlockSpec(memory_space=pltpu.VMEM)
    return pl.pallas_call(
        out_grad_kernel,
        in_specs=[pl.BlockSpec(memory_space=pltpu.SMEM), vmem, vmem, vmem],
        out_specs=vmem,
        out_shape=jax.ShapeDtypeStruct(shape, BF16),
        scratch_shapes=[pltpu.VMEM((width, res_low.shape[1]), F32)],
        compiler_params=KERNEL_PARAMS,
        cost_estimate=cost(1.8),
        name="out_gradient",
    )(ranks, attn_low, res_low, gain_terms)


def qkv_grad_kernel(shards, rank_ref, weight_ref, gain_ref, *refs):
    norms, grads = refs[:shards], refs[shards : 2 * shards]
    out_ref, norm_ref, grad_ref, flat_ref = refs[2 * shards :]
    count, columns, shard = out_ref.shape
    columns -= 1
    rows = norms[0].shape[0]
    for k in range(shards):
        norm_ref[k * rows : (k + 1) * rows] = norms[k][...]
        grad_ref[k * rows : (k + 1) * rows] = grads[k][...]
    flat_ref[...] = t_dot(grad_ref[...], norm_ref[...])
    products = matmul(weight_ref[:, : count * columns], flat_ref[...].astype(BF16))
    own = lax.broadcasted_iota(jnp.int32, (shard, shard), 0) == lax.broadcasted_iota(
        jnp.int32, (shard, shard), 1
    )
    gain = jnp.sum(jnp.where(own, products, 0.0), axis=0, keepdims=True)
    gain = (gain / gain_ref[...]).astype(BF16)
    for n in range(count):
        at = send_place(rank_ref[1] ^ n)(count)
        out_ref[at, :columns] = flat_ref[n * columns : (n + 1) * columns].astype(BF16)
        out_ref[at, columns:] = gain


def qkv_gradient(ranks, weight_low, gain_row, norms, grads, count):
    shards = len(norms)
    rows, shard = norms[0].shape
    columns = grads[0].shape[1]
    vmem = pl.BlockSpec(memory_space=pltpu.VMEM)
    return pl.pallas_call(
        functools.partial(qkv_grad_kernel, shards),
        in_specs=[pl.BlockSpec(memory_space=pltpu.SMEM)] + [vmem] * (2 + 2 * shards),
        out_specs=vmem,
        out_shape=jax.ShapeDtypeStruct((count, columns // count + 1, shard), BF16),
        scratch_shapes=[
            pltpu.VMEM((shards * rows, shard), BF16),
            pltpu.VMEM((shards * rows, columns), BF16),
            pltpu.VMEM((columns, shard), F32),
        ],
        compiler_params=KERNEL_PARAMS,
        cost_estimate=cost(2.0),
        name="qkv_gradient",
    )(ranks, weight_low, gain_row, *norms, *grads)


def feed_kernel(*refs):
    norm_refs, cot_refs, (wgu_ref, wd_ref) = refs[:SHARE], refs[SHARE : 2 * SHARE], refs[2 * SHARE : 2 * SHARE + 2]
    grad_refs = refs[2 * SHARE + 2 : 3 * SHARE + 2]
    out_refs = refs[3 * SHARE + 2 : 4 * SHARE + 2]
    inner_ref, both_ref, norm_all_ref, cot_all_ref = refs[4 * SHARE + 2 :]
    rows = norm_refs[0].shape[0]
    hidden = wd_ref.shape[0]
    for k in range(SHARE):
        norm_all_ref[k * rows : (k + 1) * rows] = norm_refs[k][...]
        cot_all_ref[k * rows : (k + 1) * rows] = cot_refs[k][...]
    gate_up_own = wgu_ref[:, : 2 * hidden]
    gate_up = matmul(norm_all_ref[...], gate_up_own)
    gate, up_part = gate_up[:, :hidden], gate_up[:, hidden:]
    sigma = 1.0 / (1.0 + jnp.exp(-gate))
    activated = gate * sigma
    inner_ref[...] = (activated * up_part).astype(BF16)
    inner_grad = dot_t(cot_all_ref[...], wd_ref[...])
    gate_grad = inner_grad * up_part * sigma * (1.0 + gate * (1.0 - sigma))
    both_ref[:, :hidden] = gate_grad.astype(BF16)
    both_ref[:, hidden:] = (inner_grad * activated).astype(BF16)
    norm_grad = dot_t(both_ref[...], gate_up_own)
    for k in range(SHARE):
        grad_refs[k][...] = norm_grad[k * rows : (k + 1) * rows].astype(grad_refs[k].dtype)
    out = matmul(inner_ref[...], wd_ref[...])
    for k in range(SHARE):
        out_refs[k][...] = out[k * rows : (k + 1) * rows].astype(out_refs[k].dtype)


def feed(norms, cots, gate_up_own, down_own):
    rows, width = norms[0].shape
    hidden = down_own.shape[0]
    shapes = [far_out((rows, width), BF16 if k else F32) for k in range(SHARE)] * 2
    shapes += [
        jax.ShapeDtypeStruct((SHARE * rows, hidden), BF16),
        jax.ShapeDtypeStruct((SHARE * rows, 2 * hidden), BF16),
        jax.ShapeDtypeStruct((SHARE * rows, width), BF16),
        jax.ShapeDtypeStruct((SHARE * rows, width), BF16),
    ]
    out = pl.pallas_call(
        feed_kernel,
        out_shape=shapes,
        compiler_params=KERNEL_PARAMS,
        cost_estimate=cost(6.4),
        name="feed",
    )(*norms, *cots, gate_up_own, down_own)
    return out[:SHARE], out[SHARE : 2 * SHARE], *out[2 * SHARE :]


def feed_grad_kernel(
    count, rank_ref, norm_ref, both_ref, cot_ref, inner_ref, after_ref, *refs
):
    del after_ref
    sides, (gate_up_ref, down_ref) = refs[:2], refs[2:]
    shards, shard = 2 * sides[0].shape[0], sides[0].shape[1]
    gate_up_cols = both_ref.shape[1]
    groups = sides[0].shape[1] // (cot_ref.shape[1] // count)
    cols = cot_ref.shape[1] // count
    gate_up_ref[...] = t_dot(norm_ref[...], both_ref[...])
    down_ref[...] = t_dot(cot_ref[...], inner_ref[...])
    for j in range(shards):
        index = rank_ref[0] ^ j
        for side in range(2):

            @pl.when(index % 2 == side)
            def _():
                part = gate_up_ref[j * shard : (j + 1) * shard]
                sides[side][index // 2, :, :gate_up_cols] = part.astype(BF16)
                for r in range(groups):
                    at = (r * shards + j) * cols
                    part = down_ref[at : at + cols].astype(BF16)
                    sides[side][index // 2, r * cols : (r + 1) * cols, gate_up_cols:] = part


def feed_gradient(ranks, norm_all, both, cot_all, inner, after, shards, count):
    width, hidden = norm_all.shape[1], inner.shape[1]
    shape = jax.ShapeDtypeStruct((shards // 2, width // shards, 3 * hidden), BF16)
    vmem = pl.BlockSpec(memory_space=pltpu.VMEM)
    return pl.pallas_call(
        functools.partial(feed_grad_kernel, count),
        in_specs=[pl.BlockSpec(memory_space=pltpu.SMEM)]
        + [vmem] * 4
        + [pl.BlockSpec(memory_space=pl.ANY)],
        out_shape=[shape, shape],
        scratch_shapes=[pltpu.VMEM((width, 2 * hidden), F32), pltpu.VMEM((width, hidden), F32)],
        compiler_params=KERNEL_PARAMS,
        cost_estimate=cost(4),
        name="feed_gradient",
    )(ranks, norm_all, both, cot_all, inner, after)


def far_sum(parts):
    low = parts[1:].astype(BF16)
    total = parts[0]
    for index in range(1, parts.shape[0]):
        total = total + flip(low[index - 1], "wa", 2 * index).astype(F32)
    return total.astype(BF16)


def rotation(positions):
    half_len = HEAD_DIM // 2
    lane = jnp.arange(PAIR, dtype=jnp.int32)
    freq = THETA ** (-(lane % half_len).astype(F32) / half_len)
    sign = jnp.where(lane % HEAD_DIM < half_len, -1.0, 1.0)
    angle = positions.astype(F32)[:, None] * freq[None, :]
    return jnp.cos(angle), jnp.sin(angle) * sign


def rms_forward(values, gain_row):
    inv_root = lax.rsqrt(jnp.mean(values * values, axis=-1, keepdims=True) + NORM_EPS)
    return (values * inv_root * gain_row, inv_root)


def rms_backward(values, inv_root, gain_row, grad_out):
    scaled = gain_row * grad_out
    return inv_root * scaled - values * inv_root**3 * jnp.mean(
        scaled * values, axis=-1, keepdims=True
    )


def adamw(weight, moment_one, moment_two, gradient, step_rate, decay_rate):
    first_new = BETA_ONE * moment_one + (1.0 - BETA_ONE) * gradient
    second_new = BETA_TWO * moment_two + (1.0 - BETA_TWO) * gradient * gradient
    first_hat = first_new / (1.0 - BETA_ONE**STEP)
    second_hat = second_new / (1.0 - BETA_TWO**STEP)
    weight_new = weight - step_rate * (
        first_hat / (jnp.sqrt(second_hat) + ADAM_EPS) + decay_rate * weight
    )
    return (weight_new, first_new, second_new)


def pick_kernel(turned, rank_ref, *refs):
    sources, outs, (flat_ref,) = refs[: len(turned)], refs[len(turned) : -1], refs[-1:]
    for source, out, turn_it in zip(sources, outs, turned):
        span = source.shape[1]
        columns = out.shape[0] if turn_it else out.shape[1]
        flat_ref[:, :span] = source[...]
        whole = flat_ref.shape[1]
        own = pltpu.roll(flat_ref[...], whole - rank_ref[1] * columns, 1)[:, :columns]
        out[...] = own.T if turn_it else own


def pick(ranks, arrays, turned, count):
    shapes = []
    for array, turn_it in zip(arrays, turned):
        rows, columns = array.shape[0], array.shape[1] // count
        shapes.append((columns, rows) if turn_it else (rows, columns))
    whole = max(-(-array.shape[1] // PAIR) * PAIR for array in arrays)
    vmem = pl.BlockSpec(memory_space=pltpu.VMEM)
    return pl.pallas_call(
        functools.partial(pick_kernel, turned),
        in_specs=[pl.BlockSpec(memory_space=pltpu.SMEM)] + [vmem] * len(arrays),
        out_shape=[jax.ShapeDtypeStruct(shape, F32) for shape in shapes],
        scratch_shapes=[pltpu.VMEM((arrays[0].shape[0], whole), F32)],
        compiler_params=KERNEL_PARAMS,
        cost_estimate=cost(1),
        name="pick",
    )(ranks, *arrays)


def update_kernel(weight_ref, first_ref, second_ref, *refs):
    parts, outs = refs[:-6], refs[-5:]
    rows, columns = weight_ref.shape
    total = sum(part[...].astype(F32) for part in parts)
    gradient = total[:rows, :columns]
    state = (weight_ref[...], first_ref[...], second_ref[...])
    values = adamw(*state, gradient, RATE_MATRIX, WEIGHT_DECAY)
    for out, value in zip(outs, (*values, gradient)):
        out[...] = value
    if total.shape[0] > rows:
        outs[4][...] = total[rows:]
    elif total.shape[1] > columns:
        outs[4][...] = total[:, columns:]


def update(weight, first, second, parts, after):
    rows, columns = weight.shape
    rest = (1, columns) if parts[0].shape[0] > rows else (rows, 1)
    shapes = [jax.ShapeDtypeStruct(weight.shape, F32)] * 4 + [jax.ShapeDtypeStruct(rest, F32)]
    return pl.pallas_call(
        update_kernel,
        in_specs=[pl.BlockSpec(memory_space=pltpu.VMEM)] * (3 + len(parts))
        + [pl.BlockSpec(memory_space=pl.ANY)],
        out_shape=shapes,
        compiler_params=KERNEL_PARAMS,
        cost_estimate=cost(1.5),
        name="update",
    )(weight, first, second, *parts, after)


def own_columns(array, ctx_rank, ctx_count):
    col_width = array.shape[1] // ctx_count
    return lax.dynamic_slice_in_dim(array, ctx_rank * col_width, col_width, 1)


def local(
    layer_input,
    cotangent,
    block_order,
    qkv_weight,
    qkv_first,
    qkv_second,
    out_weight,
    out_first,
    out_second,
    gate_up_weight,
    gate_up_first,
    gate_up_second,
    down_weight,
    down_first,
    down_second,
    gains,
    gain_first,
    gain_second,
):
    ctx_rank = lax.axis_index("ctx")
    ctx_count = lax.axis_size("ctx")
    wa_rank = lax.axis_index("wa")
    wa_count = lax.axis_size("wa")
    place = ctx_rank % SHARE
    tokens = layer_input[0]
    upstream = cotangent[0]
    tok_rows, width = tokens.shape
    shard = width // wa_count
    hidden = FF // SHARE
    query_width = HEADS * HEAD_DIM
    pair_width = KV_HEADS * HEAD_DIM
    half_len = tok_rows // 2

    gains_low = gains.astype(BF16)
    qkv_low = pack(qkv_weight, gains)
    far = wa_count // 2
    qkv_far = flip(qkv_low, "wa", far)
    cot_low, qkv_near = lax.optimization_barrier((upstream.astype(BF16), flip(qkv_low, "wa", 1)))
    cots = share_gather(cot_low)
    out_low = out_weight.astype(BF16)
    gate_up_low = jnp.concatenate(
        [
            lax.dynamic_slice_in_dim(gate_up_weight, place * hidden, hidden, 1),
            lax.dynamic_slice_in_dim(gate_up_weight, FF + place * hidden, hidden, 1),
        ],
        axis=1,
    ).astype(BF16)
    down_rows = FF // wa_count // SHARE
    down_low = lax.dynamic_slice_in_dim(down_weight, place * down_rows, down_rows, 0).astype(BF16)
    ranks = jnp.stack([wa_rank, ctx_rank]).astype(jnp.int32)

    order = block_order[0].reshape(ctx_count, 2)
    offsets = jnp.arange(half_len, dtype=jnp.int32)
    key_starts = order[ctx_rank ^ jnp.array(pair_offsets(), jnp.int32)]
    key_pos = (key_starts[:, :, None] * half_len + offsets).reshape(-1)
    own_pos = key_pos[:tok_rows]
    starts = key_starts[0]
    cos_lanes, sin_lanes = rotation(own_pos)

    both_low = jnp.concatenate([gate_up_low, out_low], axis=1)
    first = (qkv_far, cots, both_low, down_low, cos_lanes, sin_lanes, tokens, key_pos, starts)
    first = lax.optimization_barrier(first)
    qkv_far, cots, both_low, down_low, cos_lanes, sin_lanes, tokens, key_pos, starts = first
    qkv_blocks = {0: qkv_low, far: qkv_far}
    for bit in reversed(bits_of(far)):
        qkv_blocks.update({key | bit: flip(qkv_blocks[key], "wa", bit) for key in list(qkv_blocks)})
    qkv_blocks[1] = qkv_near
    both_full = lax.all_gather(both_low, "wa", axis=0, tiled=True)
    down_low = swap_places(down_low)

    query_low, pair_low, norm_cols, root_one, gain_norm, qkv_full = project(
        ranks, tokens, cos_lanes, sin_lanes, [qkv_blocks[k] for k in range(wa_count)]
    )

    pair_low, down_low = lax.optimization_barrier((pair_low, down_low))
    pairs = pair_gather(pair_low)
    pairs, down_low = lax.optimization_barrier((pairs, down_low))
    down_own = lax.all_gather(down_low, "wa", axis=0, tiled=True)
    attn, log_total, attn_low, residual, norm_two_low, root_two = attend(
        query_low, pairs, starts, key_pos, tokens, gain_norm, both_full
    )

    norms = share_gather(norm_two_low)
    norm_rows = [norm_cols[0]] + [flip(norm_cols[k], "wa", k) for k in range(1, wa_count)]
    norms, norm_rows = lax.optimization_barrier((norms, norm_rows))
    grads, outs, inner_low, gate_up_grad_low, norm_two_all, cot_all = feed(
        norms, cots, both_full, down_own
    )
    grads = [grads[0]] + share_send(grads[1:])
    feed_keep, feed_send = feed_gradient(
        ranks,
        norm_two_all,
        gate_up_grad_low,
        cot_all,
        inner_low,
        grads[1],
        wa_count,
        ctx_count,
    )
    grads, feed_keep, feed_send = lax.optimization_barrier((grads, feed_keep, feed_send))
    feed_sum = feed_keep.astype(F32) + flip(feed_send, "wa", 1).astype(F32)
    outs = [outs[0]] + share_send(outs[1:])

    residual_grad, res_low, query_grad, gain_terms, pair_parts = attend_back(
        grads,
        residual,
        root_two,
        gain_norm,
        upstream,
        both_full,
        query_low,
        attn,
        log_total,
        pairs,
        starts,
        key_pos,
        cos_lanes,
        sin_lanes,
    )
    pair_parts, outs = lax.optimization_barrier((pair_parts, outs))
    feed_sum = far_sum(feed_sum)
    feed_sum, pair_terms = pair_reduce(pair_parts, feed_sum)
    out_parts = out_gradient(ranks, attn_low, res_low, gain_terms, wa_count, ctx_count)
    out_keep = out_parts[: wa_count // 2]
    out_got = flip(out_parts[wa_count // 2 :], "wa", 1)
    projected_grad_low = join(query_grad, cos_lanes, sin_lanes, pair_terms)

    projected_grad_low, late_ranks = lax.optimization_barrier((projected_grad_low, ranks))
    grads_far = flip(projected_grad_low, "wa", far)
    states = pick(
        late_ranks,
        (qkv_weight, qkv_first, qkv_second, out_weight, out_first, out_second),
        (True, True, True, False, False, False),
        ctx_count,
    )
    held = (grads_far, out_keep, out_got, states)
    grads_far, out_keep, out_got, states = lax.optimization_barrier(held)
    grad_blocks = {0: projected_grad_low, far: grads_far}
    for bit in reversed(bits_of(far)):
        grad_blocks.update({key | bit: flip(grad_blocks[key], "wa", bit) for key in list(grad_blocks)})
    grad_rows = [grad_blocks[k] for k in range(wa_count)]
    out_sum = out_keep.astype(F32) + out_got.astype(F32)
    out_low = out_sum.astype(BF16)
    out_terms = [out_sum[0]]
    out_terms += [flip(out_low[j], "wa", 2 * j) for j in range(1, wa_count // 2)]
    qkv_parts = qkv_gradient(
        ranks, qkv_low, gains_low[0:1].astype(F32), norm_rows, grad_rows, ctx_count
    )
    held = (qkv_parts, feed_sum, projected_grad_low, residual_grad)
    qkv_parts, feed_sum, projected_grad_low, residual_grad = lax.optimization_barrier(held)
    near, qkv_parts = pieces_parts(qkv_parts, "ctx")
    norm_one_grad = dot_t(projected_grad_low, qkv_full)
    input_grad = residual_grad + rms_backward(tokens, root_one, gain_norm[0], norm_one_grad)
    gate_up_parts, down_parts = [feed_sum[:, : 2 * hidden]], [feed_sum[:, 2 * hidden :]]
    for bit in reversed(far_bits()):
        gate_up_sum = sum(part.astype(F32) for part in gate_up_parts).astype(BF16)
        down_sum = sum(part.astype(F32) for part in down_parts).astype(BF16)
        half, rows = gate_up_sum.shape[1] // 2, down_sum.shape[0] // 2
        side = ((ctx_rank & bit) != 0).astype(jnp.int32)
        gate_up_mine = lax.dynamic_slice_in_dim(gate_up_sum, side * half, half, 1)
        down_mine = lax.dynamic_slice_in_dim(down_sum, side * rows, rows, 0)
        gate_up_other = lax.dynamic_slice_in_dim(gate_up_sum, (1 - side) * half, half, 1)
        down_other = lax.dynamic_slice_in_dim(down_sum, (1 - side) * rows, rows, 0)
        gate_up_parts = [gate_up_mine, flip(gate_up_other, "ctx", bit)]
        down_parts = [down_mine, flip(down_other, "ctx", bit)]
    groups = ctx_count // SHARE
    moves = []
    for ctx in range(ctx_count):
        high, low = ctx // SHARE, ctx % SHARE
        per_half = groups // 2
        moves.append((ctx, ((high // per_half) * SHARE + low) * per_half + high % per_half))
    if any(source != target for source, target in moves):
        gate_up_sum = sum(part.astype(F32) for part in gate_up_parts).astype(BF16)
        gate_up_parts = [lax.ppermute(gate_up_sum, "ctx", moves)]
    out_sum = sum(part.astype(F32) for part in out_terms).astype(BF16)
    down_sum = swap_places(sum(part.astype(F32) for part in down_parts).astype(BF16))
    _, out_parts = pieces_parts(out_sum, "ctx")
    layer_output = residual + sum(part.astype(F32) for part in outs)


    def state_of(*arrays):
        return [own_columns(array, ctx_rank, ctx_count) for array in arrays]

    gate_up_sum = sum(part.astype(F32) for part in gate_up_parts)
    down_sum = down_sum.astype(F32)
    gate_up_values = adamw(
        *state_of(gate_up_weight, gate_up_first, gate_up_second),
        gate_up_sum,
        RATE_MATRIX,
        WEIGHT_DECAY,
    )
    down_state = [array.T for array in state_of(down_weight, down_first, down_second)]
    down_values = adamw(*down_state, down_sum, RATE_MATRIX, WEIGHT_DECAY)
    *out_values, out_sum, gain_two_sum = update(*states[3:], out_parts, near)
    *qkv_values, qkv_sum, gain_one_sum = update(*states[:3], qkv_parts, near)
    gain_sum = jnp.stack([gain_one_sum[0], gain_two_sum[:, 0]])
    updates = [value.T for value in qkv_values]
    updates += [*out_values, *gate_up_values]
    updates += [value.T for value in down_values]
    updates += adamw(gains, gain_first, gain_second, gain_sum, RATE_GAIN, 0.0)
    sums = [qkv_sum.T, out_sum, gate_up_sum, down_sum.T]
    return (
        layer_output[None],
        input_grad[None],
        *updates,
        *sums,
        gain_sum,
    )


def solution(mesh):
    rows = P("wa", None)
    tokens = P("wa", "ctx", None)
    piece = P("wa", "ctx")
    gain = P(None, "wa")
    return jax.shard_map(
        local,
        mesh=mesh,
        in_specs=(tokens, tokens) + (rows,) * 13 + (gain,) * 3,
        out_specs=(tokens, tokens) + (piece,) * 12 + (gain,) * 3 + (piece,) * 4 + (gain,),
        check_vma=False,
    )
```
